32 devices in a mesh: ra: 8 (over y, x, core), dec: 4 (over z).
Axes of the slice: x: 2, y: 2, z: 4, core: 2. Of those that a mesh axis runs over, the one named last changes fastest.
Arguments:
- log_flux: float32 [5, 8192], P(None, ('ra', 'dec')), may hold values from 5.5 to 9.5
- position: float32 [2, 8192], P(None, ('ra', 'dec')), may hold values from 0 to 640
- log_width: float32 [8192], P(('ra', 'dec')), may hold values from -3.5 to -0.5
- owner_tile: int32 [8192, 1], P(('ra', 'dec')), may hold values from 0 to 31; in each aligned block of 256 rows (0 to 255, 256 to 511, ...) at most 16 rows name the same one
- sky_level: float32 [8, 4, 5], P('ra', 'dec'), may hold values from 0.5 to 4
- counts: int32 [5, 5120, 2560], P(None, 'ra', 'dec'), may hold values from 0 to 7
Outputs:
- gradient: float32 [8, 8192], P(None, ('ra', 'dec'))
The draws below stay inside these ranges and needn't reach their ends.
Inputs may be any that keep to these rules, and one draw needn't show every extreme that they name: `owner_tile`: in each aligned block of 256 catalog rows (the rows of one device) no tile is named more than 16 times, a bound that some block reaches.
All inputs are finite; a program needn't handle non-finite values.
Results may differ from the reference program's by a relative error of at most 0.00095.
Values may be sent and summed in bfloat16 or wider, within the bound.
No kernel may reach another device: no remote copies, remote signals or barrier semaphores. Data moves between devices by JAX's collectives and lax.ppermute only.
A program may use at most 128 MiB of HBM per device.

```python
import math
import jax
import jax.numpy as jnp
import numpy as np
from jax import lax

BANDS = 5
TILE = 640
MARGIN = 128
CAT_DEV = 256
TILES = 32
CAP = 16
SLOTS = 512
CANVAS = 896
CAT = 8192
SKY_RA = 5120
SKY_DEC = 2560
N_RA = 8
N_DEC = 4


def draw_position(key, part):
    uniform_part = jax.random.uniform(jax.random.fold_in(key, 11), (2, CAT), jnp.float32)
    centered = 2.0 * uniform_part - 1.0
    power = 0.5
    warped = jnp.where(centered >= 0.0, 1.0, -1.0) * jnp.abs(centered) ** power
    return jnp.clip(0.5 * TILE * (1.0 + warped), 0.0, 1.0 * TILE).astype(jnp.float32)


def draw_counts(key, part):
    top_count = 4 + 6400 * CAT_DEV // (TILE * TILE)
    region_rows = (SKY_RA + MARGIN - 1) // MARGIN
    region_cols = (SKY_DEC + MARGIN - 1) // MARGIN
    phase_rows = jax.random.randint(jax.random.fold_in(key, 21), (BANDS, region_rows, region_cols), 0, 4)
    phase_cols = jax.random.randint(jax.random.fold_in(key, 22), (BANDS, region_rows, region_cols), 0, 4)
    phase_rows = jnp.repeat(jnp.repeat(phase_rows, MARGIN, axis=1), MARGIN, axis=2)[:, :SKY_RA, :SKY_DEC]
    phase_cols = jnp.repeat(jnp.repeat(phase_cols, MARGIN, axis=1), MARGIN, axis=2)[:, :SKY_RA, :SKY_DEC]
    pixel_rows = jnp.arange(SKY_RA, dtype=jnp.int32)[None, :, None]
    pixel_cols = jnp.arange(SKY_DEC, dtype=jnp.int32)[None, None, :]
    bright = ((pixel_rows + phase_rows) % 4 >= 2) | ((pixel_cols + phase_cols) % 4 >= 2)
    noise = jax.random.randint(jax.random.fold_in(key, 23), (BANDS, SKY_RA, SKY_DEC), 0, top_count // 4 + 1)
    return jnp.where(bright, top_count - 1 - noise, noise).astype(jnp.int32)


def levels(key, shape, split, smallest, high):
    def one(dim, blocks):
        heights = jax.random.uniform(jax.random.fold_in(jax.random.fold_in(key, 6), dim), (blocks,), jnp.float32, smallest / len(split), high / len(split))
        return jnp.repeat(jnp.exp(heights), shape[dim] // blocks).reshape((-1,) + (1,) * (len(shape) - dim - 1))

    gain = one(*split[0])
    for cut in split[1:]:
        gain = gain * one(*cut)
    return gain


def routed_block(key, own, number, rows, count, top, bound, lean):
    ranking = jax.random.permutation(key, count)
    crowded, usual = shares(count, rows * top, bound, lean, True), shares(count, rows * top, bound, lean, False)
    places = jnp.arange(count)

    def named(tallies, offset_by):
        used = int((tallies > 0).sum())
        fixed = max(1, used // 4)
        shifted = fixed + (places - fixed + offset_by * (used - fixed)) % max(1, count - fixed)
        return jnp.zeros((count,), jnp.int32).at[ranking[jnp.where(places < fixed, places, shifted)]].set(jnp.asarray(tallies, jnp.int32))

    tallies = jnp.where(number % 4 == 0, named(crowded, number // 4), named(usual, number - number // 4 - 1))
    mixed = jax.random.permutation(jax.random.fold_in(own, 3), count)
    donor, receiver = mixed[0:count // 2 * 2:2], mixed[1:count // 2 * 2:2]
    slack = jnp.minimum(tallies[donor] - 1, bound - tallies[receiver]) // 2
    slack = jnp.where((donor == ranking[0]) | (receiver == ranking[0]) | (tallies[receiver] == 0), 0, jnp.maximum(slack, 0))
    shifted = jax.random.randint(jax.random.fold_in(own, 4), (count // 2,), 0, 1 << 20) % (slack + 1)
    tallies = tallies.at[donor].add(-shifted).at[receiver].add(shifted)
    members = jnp.searchsorted(jnp.cumsum(tallies), jnp.arange(rows * top), side="right").astype(jnp.int32)
    table = members.reshape(top, rows).T
    table = table[jax.random.permutation(jax.random.fold_in(own, 1), rows)]
    offset_by = jax.random.randint(jax.random.fold_in(own, 2), (rows, 1), 0, top)
    return jnp.take_along_axis(table, (jnp.arange(top)[None, :] + offset_by) % top, axis=1)


def shares(number_of, total, limit, skew, full):
    weights = [(1 << 20) // math.isqrt(rank ** skew) + 1 for rank in range(1, number_of + 1)]
    largest = limit if full else min(limit, max(-(-total // number_of), total * weights[0] // sum(weights)))
    least = 1 if total - largest >= number_of - 1 else 0
    holding, surplus = [largest] + [least] * (number_of - 1), total - largest - least * (number_of - 1)
    while surplus > 0:
        movable = [i for i in range(1, number_of) if holding[i] < largest] or [i for i in range(1, number_of) if holding[i] < limit]
        pool, left = sum([weights[i] for i in movable]), surplus
        for i in movable:
            more = min(limit - holding[i], max(1, left * weights[i] // pool), surplus)
            holding[i] = holding[i] + more
            surplus = surplus - more
    return np.array(holding)


def setup_inputs(seed: int = 0) -> dict:
    key_of = jax.random.split(jax.random.key(seed), 7)
    log_flux = jnp.clip(5.5 + 4.0 * jax.random.uniform(key_of[0], (BANDS, CAT), jnp.float32) ** levels(key_of[0], (BANDS, CAT), ((1, 32),), -0.2, 0.2), 5.5, 9.5)
    position = draw_position(jax.random.fold_in(key_of[6], 71), 0)
    log_width = jnp.clip(-3.5 + 3.0 * jax.random.uniform(key_of[2], (CAT,), jnp.float32) ** levels(key_of[2], (CAT,), ((0, 32),), -0.2, 0.2), -3.5, -0.5)
    owner_tile_keys = jax.random.split(jax.random.fold_in(key_of[3], 1), CAT // CAT_DEV)
    owner_tile_turns = jax.random.permutation(jax.random.fold_in(key_of[3], 3), CAT // CAT_DEV)
    owner_tile = jax.vmap(lambda own, number: routed_block(jax.random.fold_in(key_of[3], 2), own, number, CAT_DEV, TILES, 1, CAP, 2))(owner_tile_keys, owner_tile_turns).reshape((CAT, 1))
    sky_level = jnp.clip(jnp.exp(math.log(4.0) - 2.0794415 * jax.random.uniform(key_of[4], (N_RA, N_DEC, BANDS), jnp.float32) ** levels(key_of[4], (N_RA, N_DEC, BANDS), ((0, 8), (1, 4)), -0.2, 0.2)), 0.5, 4.0)
    counts = draw_counts(jax.random.fold_in(key_of[6], 71), 0)
    return dict(log_flux=log_flux, position=position, log_width=log_width, owner_tile=owner_tile, sky_level=sky_level, counts=counts)


def profiles(center, log_width):
    coords = jnp.arange(CANVAS, dtype=jnp.float32) - MARGIN + 0.5
    sigma = MARGIN * jnp.exp(log_width)
    offset = (coords[:, None] - center[None, :]) / sigma[None, :]
    shape = jnp.exp(-0.5 * offset * offset) / (math.sqrt(2.0 * math.pi) * sigma[None, :])
    return (shape, offset, sigma)

def render(arrived):
    flux_values = arrived[8][None, :] * jnp.exp(arrived[0:5])
    row_prof, _, _ = profiles(arrived[5], arrived[7])
    col_prof, _, _ = profiles(arrived[6], arrived[7])
    scaled = (row_prof[None, :, :] * flux_values[:, None, :]).astype(jnp.bfloat16)
    col_bf = col_prof.astype(jnp.bfloat16)
    canvas = jnp.einsum('bis,js->bij', scaled.astype(jnp.float32), col_bf.astype(jnp.float32))
    return canvas.astype(jnp.bfloat16)

def tile_grads(arrived, weight_canvas):
    flux_values = arrived[8][None, :] * jnp.exp(arrived[0:5])
    row_prof, row_off, sigma = profiles(arrived[5], arrived[7])
    col_prof, col_off, _ = profiles(arrived[6], arrived[7])
    row_bf = row_prof.astype(jnp.bfloat16).astype(jnp.float32)
    col_bf = col_prof.astype(jnp.bfloat16).astype(jnp.float32)
    wfloat = weight_canvas.astype(jnp.float32)
    along_rows = jnp.einsum('bij,js->bis', wfloat, col_bf)
    along_cols = jnp.einsum('bij,is->bjs', wfloat, row_bf)
    flux_grad = flux_values * lax.optimization_barrier(jnp.sum(row_bf[None, :, :] * along_rows, axis=1))
    row_total = lax.optimization_barrier(jnp.sum(flux_values[:, None, :] * along_rows, axis=0))
    col_total = lax.optimization_barrier(jnp.sum(flux_values[:, None, :] * along_cols, axis=0))
    row_grad = lax.optimization_barrier(jnp.sum(row_prof * row_off / sigma[None, :] * row_total, axis=0))
    col_grad = lax.optimization_barrier(jnp.sum(col_prof * col_off / sigma[None, :] * col_total, axis=0))
    width_grad = lax.optimization_barrier(jnp.sum(row_prof * (row_off * row_off - 1.0) * row_total, axis=0)) + lax.optimization_barrier(jnp.sum(col_prof * (col_off * col_off - 1.0) * col_total, axis=0))
    return jnp.concatenate([flux_grad, row_grad[None], col_grad[None], width_grad[None]], axis=0)

def reference(log_flux, position, log_width, owner_tile, sky_level, counts):
    params = jnp.concatenate([log_flux, position, log_width[None, :], jnp.ones((1, CAT), jnp.float32)], axis=0)
    target_tile = owner_tile[:, 0]
    blocks = target_tile.reshape(TILES, CAT_DEV)
    matches = blocks[:, None, :] == blocks[:, :, None]
    order = jnp.arange(CAT_DEV, dtype=jnp.int32)
    earlier = order[None, :] < order[:, None]
    rank_in = lax.optimization_barrier(jnp.sum((matches & earlier[None]).astype(jnp.int32), axis=2)).reshape(CAT)
    slot_of = jnp.arange(CAT, dtype=jnp.int32) // CAT_DEV * CAP + rank_in
    arrived = jnp.zeros((TILES, 9, SLOTS), jnp.float32).at[target_tile, :, slot_of].set(params.T)

    def add_tile(padded, tile_index):
        ra_index = (tile_index // N_DEC).astype(jnp.int32)
        dec_index = (tile_index % N_DEC).astype(jnp.int32)
        canvas = render(arrived[tile_index])
        piece = lax.optimization_barrier(canvas).astype(jnp.float32)
        starts = (jnp.int32(0), ra_index * TILE, dec_index * TILE)
        region = lax.dynamic_slice(padded, starts, (BANDS, CANVAS, CANVAS))
        return (lax.dynamic_update_slice(padded, region + piece, starts), None)
    padded, _ = lax.scan(add_tile, jnp.zeros((BANDS, SKY_RA + 2 * MARGIN, SKY_DEC + 2 * MARGIN), jnp.float32), jnp.arange(TILES, dtype=jnp.int32))
    sky_model = padded[:, MARGIN:MARGIN + SKY_RA, MARGIN:MARGIN + SKY_DEC].reshape(BANDS, N_RA, TILE, N_DEC, TILE)
    background = jnp.transpose(sky_level, (2, 0, 1))[:, :, None, :, None]
    intensity = (sky_model + background).reshape(BANDS, SKY_RA, SKY_DEC)
    weights = (counts.astype(jnp.float32) / intensity - 1.0).astype(jnp.bfloat16)
    wpadded = jnp.pad(weights, ((0, 0), (MARGIN, MARGIN), (MARGIN, MARGIN)))

    def one_tile(tile_index):
        ra_index = (tile_index // N_DEC).astype(jnp.int32)
        dec_index = (tile_index % N_DEC).astype(jnp.int32)
        window = lax.dynamic_slice(wpadded, (jnp.int32(0), ra_index * TILE, dec_index * TILE), (BANDS, CANVAS, CANVAS))
        return tile_grads(arrived[tile_index], window)
    slot_grad = lax.map(one_tile, jnp.arange(TILES, dtype=jnp.int32))
    return slot_grad[target_tile, :, slot_of].T
```

```python
import functools
import math

import jax
import jax.numpy as jnp
from jax import lax
from jax.experimental import pallas as pl
from jax.experimental.pallas import tpu as pltpu
from jax.sharding import PartitionSpec as P

MARGIN = 128
CAT_DEV = 256
BANDS = 5
AXES = ("ra", "dec")
AROUND = [(0, 0), (-1, 0), (1, 0), (0, -1), (0, 1), (-1, -1), (-1, 1), (1, -1), (1, 1)]
EMPTY = -1e30
K = math.sqrt(0.5 * math.log2(math.e))
K2 = 2.0 * math.log(2.0)
F32 = jnp.float32
BF16 = jnp.bfloat16


def dot(a, b):
    return jnp.dot(a, b, preferred_element_type=F32)


def coords(length, first, axis):
    shape = (length, 1) if axis == 0 else (1, length)
    return lax.broadcasted_iota(jnp.int32, shape, axis).astype(F32) + (first + 0.5)


def shape_of(x, center, scale, norm):
    t = (x - center) * scale
    return jnp.exp2(-(t * t)) * norm, t


def params(table, axis):
    def pick(i):
        return table[i : i + 1, :] if axis == 0 else table[:, i : i + 1]

    flux = [jnp.exp(pick(b)) for b in range(BANDS)]
    inverse = jnp.exp(-pick(7)) * (1.0 / MARGIN)
    return flux, pick(5), pick(6), inverse * K, inverse * (1.0 / math.sqrt(2.0 * math.pi)), inverse


def moments(total, x, center, scale, norm, axis):
    p, t = shape_of(x, center, scale, norm)
    q = p * total
    q1 = q * t
    q2 = q1 * t
    return q, q1, q2


def core(side, slots, prm, sky, counts_hbm, out, counts, acc, w, wedge, c_row, c_sc, c_scT, c_col, c_colT,
         v_row, v_sc, v_scT, v_col, v_colT, h_row, h_rowT, h_sc, h_scT, h_colT,
         k_row, k_rowT, k_sc, k_scT, k_colT, big, gsum, hsum, sem):
    M = MARGIN
    rim = side - M
    fetch = pltpu.make_async_copy(counts_hbm, counts, sem)
    fetch.start()

    def table_of(n):
        rows = prm[n]
        return rows, rows.T

    def firsts(di, dj):
        return -di * side, -dj * side

    def span(d):
        return (0, side) if d == 0 else ((0, M) if d < 0 else (rim, M))

    def fill(n, row_at, row_len, col_at, col_len, first_r, first_c, row, rowT, col, colT, scR, scRT, scC, scCT):
        rows, cols = table_of(n)
        flux, rc, cc, scale, norm, _ = params(rows, 0)
        fluxT, rcT, ccT, scaleT, normT, _ = params(cols, 1)
        step = 128

        def by_rows(i, _):
            at = pl.multiple_of(i * step, step)
            p, _t = shape_of(coords(step, (row_at + first_r + i * step).astype(F32), 0), rc, scale, norm)
            if row is not None:
                row[pl.ds(at, step), :] = p.astype(BF16)
            if scR is not None:
                for b in range(BANDS):
                    scR[pl.ds(pl.multiple_of(b * row_len + i * step, step), step), :] = (p * flux[b]).astype(BF16)
            p, _t = shape_of(coords(step, (row_at + first_r + i * step).astype(F32), 1), rcT, scaleT, normT)
            if rowT is not None:
                rowT[:, pl.ds(at, step)] = p.astype(BF16)
            if scRT is not None:
                for b in range(BANDS):
                    scRT[:, pl.ds(pl.multiple_of(b * row_len + i * step, step), step)] = (p * fluxT[b]).astype(BF16)
            return 0

        lax.fori_loop(0, row_len // step, by_rows, 0)

        def by_cols(i, _):
            at = pl.multiple_of(i * step, step)
            p, _t = shape_of(coords(step, (col_at + first_c + i * step).astype(F32), 0), cc, scale, norm)
            if col is not None:
                col[pl.ds(at, step), :] = p.astype(BF16)
            if scC is not None:
                for b in range(BANDS):
                    scC[pl.ds(pl.multiple_of(b * col_len + i * step, step), step), :] = (p * flux[b]).astype(BF16)
            p, _t = shape_of(coords(step, (col_at + first_c + i * step).astype(F32), 1), ccT, scaleT, normT)
            if colT is not None:
                colT[:, pl.ds(at, step)] = p.astype(BF16)
            if scCT is not None:
                for b in range(BANDS):
                    scCT[:, pl.ds(pl.multiple_of(b * col_len + i * step, step), step)] = (p * fluxT[b]).astype(BF16)
            return 0

        lax.fori_loop(0, col_len // step, by_cols, 0)

    zero = jnp.int32(0)
    fill(0, zero, side, zero, side, zero, zero, c_row, None, c_col, c_colT, c_sc, c_scT, None, None)

    def own_band(b, _):
        at = pl.multiple_of(b * side, 128)
        acc[b] = dot(c_sc[pl.ds(at, side), :], c_colT[...])
        return 0

    lax.fori_loop(0, BANDS, own_band, 0)

    def upright(v, _):
        d = 2 * v - 1
        at = pl.multiple_of(v * rim, 128)
        fill(1 + v, at, M, zero, side, -d * side, zero, v_row.at[v], None, v_col.at[v], v_colT.at[v],
             v_sc.at[v], v_scT.at[v], None, None)
        big[...] = dot(v_sc[v], v_colT[v])
        for b in range(BANDS):
            acc[b, pl.ds(at, M), :] += big[b * M : (b + 1) * M, :]
        return 0

    lax.fori_loop(0, 2, upright, 0)

    def sideways(v, _):
        d = 2 * v - 1
        at = pl.multiple_of(v * rim, 128)
        fill(3 + v, zero, side, at, M, zero, -d * side, h_row.at[v], h_rowT.at[v], None, h_colT.at[v],
             None, None, h_sc.at[v], h_scT.at[v])
        big[...] = dot(h_row[v], h_scT[v])
        for b in range(BANDS):
            acc[b, :, pl.ds(at, M)] += big[:, b * M : (b + 1) * M]
        return 0

    lax.fori_loop(0, 2, sideways, 0)

    def corner(v, _):
        vr, vc = v // 2, v % 2
        at_r = pl.multiple_of(vr * rim, 128)
        at_c = pl.multiple_of(vc * rim, 128)
        fill(5 + v, at_r, M, at_c, M, (1 - 2 * vr) * side, (1 - 2 * vc) * side, k_row.at[v], k_rowT.at[v], None,
             k_colT.at[v], None, None, k_sc.at[v], k_scT.at[v])
        big[:M] = dot(k_row[v], k_scT[v])
        for b in range(BANDS):
            acc[b, pl.ds(at_r, M), pl.ds(at_c, M)] += big[:M, b * M : (b + 1) * M]
        return 0

    lax.fori_loop(0, 4, corner, 0)

    fetch.wait()

    for b in range(BANDS):
        level = sky[0, 0, b]

        def band_rows(i, _):
            rows = pl.ds(pl.multiple_of(i * 64, 64), 64)
            ratio = counts[b, rows, :].astype(F32) / (acc[b, rows, :] + level)
            weights = (ratio - 1.0).astype(BF16)
            w[b, rows, :] = weights
            wedge[0, rows, b * M : (b + 1) * M] = weights[:, :M]
            wedge[1, rows, b * M : (b + 1) * M] = weights[:, rim:]
            return 0

        lax.fori_loop(0, side // 64, band_rows, 0)

    def reduce_rows(n, first, length):
        _, rc, _, scale, norm, inverse = params(prm[n], 0)

        def step(i, sums):
            at = pl.multiple_of(i * 64, 64)
            x = coords(64, (first + i * 64).astype(F32), 0)
            q = moments(gsum[pl.ds(at, 64), :], x, rc, scale, norm, 0)
            return tuple(s + jnp.sum(v.reshape(8, 8, slots), axis=0) for s, v in zip(sums, q))

        s0, s1, s2 = lax.fori_loop(0, length // 64, step, (jnp.zeros((8, slots), F32),) * 3)
        s0, s1, s2 = [jnp.sum(s, axis=0, keepdims=True) for s in (s0, s1, s2)]
        return s1 * inverse * (1.0 / K), s2 * K2 - s0

    def reduce_cols(n, first, length, source, extra):
        cols = prm[n].T
        _, _, cc, scale, norm, inverse = params(cols, 1)
        s0 = jnp.zeros((slots, 128), F32)
        s1, s2 = s0, s0
        for i in range(length // 128):
            x = coords(128, first + i * 128, 1)
            q = moments(source[:, i * 128 : (i + 1) * 128], x, cc, scale, norm, 1)
            s0, s1, s2 = s0 + q[0], s1 + q[1], s2 + q[2]
        total = [jnp.sum(s, axis=1, keepdims=True) for s in (s0, s1, s2)]
        lane = lax.broadcasted_iota(jnp.int32, (1, 128), 1)
        found = jnp.where(lane == 6, total[1] * inverse * (1.0 / K), 0.0)
        found = found + jnp.where(lane == 7, total[2] * K2 - total[0], 0.0)
        for m, e in extra:
            found = found + jnp.where(lane == m, e, 0.0)
        return found.T[:8]

    def finish(n, rows, found):
        out[n] = jnp.concatenate(rows, axis=0) + found

    nothing = jnp.zeros((1, slots), F32)

    fl0, _, _, _, _, _ = params(prm[0], 0)
    gsum[...] = jnp.zeros_like(gsum)
    hsum[...] = jnp.zeros_like(hsum)

    own = []
    for b in range(BANDS):
        big[:, :slots] = dot(w[b], c_col[...])

        def own_rows(i, s):
            rows = pl.ds(pl.multiple_of(i * 64, 64), 64)
            a = big[rows, :slots]
            gsum[rows, :] += a * fl0[b]
            return s + jnp.sum((a * c_row[rows, :].astype(F32)).reshape(8, 8, slots), axis=0)

        s = lax.fori_loop(0, side // 64, own_rows, jnp.zeros((8, slots), F32))
        own.append(jnp.sum(s, axis=0, keepdims=True) * fl0[b])
        hsum[...] += dot(c_scT[:, b * side : (b + 1) * side], w[b])
    row_grad, width_r = reduce_rows(0, zero, side)
    found = reduce_cols(0, zero.astype(F32), side, hsum, [])
    finish(0, own + [row_grad, nothing, width_r], found)

    def upright_adjoint(v, _):
        d = 2 * v - 1
        n = 1 + v
        at = pl.multiple_of(v * rim, 128)
        strip = w[:, pl.ds(at, M), :].reshape(BANDS * M, side)
        big[:, :slots] = dot(strip, v_col[v])
        hsum[...] = dot(v_scT[v], strip)
        flux, _, _, _, _, _ = params(prm[n], 0)
        sums = []
        gsum[:M] = jnp.zeros((M, slots), F32)
        for b in range(BANDS):
            a = big[b * M : (b + 1) * M, :slots]
            gsum[:M] += a * flux[b]
            sums.append(jnp.sum(a * v_row[v].astype(F32), axis=0, keepdims=True) * flux[b])
        row_grad, width_r = reduce_rows(n, at - d * side, M)
        found = reduce_cols(n, zero.astype(F32), side, hsum, [])
        finish(n, sums + [row_grad, nothing, width_r], found)
        return 0

    lax.fori_loop(0, 2, upright_adjoint, 0)

    def flat_adjoint(n, strip, rowT, sc, colT, first_r, length, first_c):
        hsum[...] = dot(rowT, strip)
        gsum[:length] = dot(strip, sc)
        fluxT = params(prm[n].T, 1)[0]
        shape = colT.astype(F32)
        total = jnp.zeros((slots, M), F32)
        extra = []
        for b in range(BANDS):
            a = hsum[:, b * M : (b + 1) * M]
            total = total + a * fluxT[b]
            extra.append((b, jnp.sum(a * shape, axis=1, keepdims=True) * fluxT[b]))
        row_grad, width_r = reduce_rows(n, first_r, length)
        hsum[:, :M] = total
        found = reduce_cols(n, first_c, M, hsum, extra)
        finish(n, [nothing] * BANDS + [row_grad, nothing, width_r], found)

    def sideways_adjoint(v, _):
        d = 2 * v - 1
        at = v * rim
        flat_adjoint(3 + v, wedge[v], h_rowT[v], h_sc[v], h_colT[v], zero, side, (at - d * side).astype(F32))
        return 0

    lax.fori_loop(0, 2, sideways_adjoint, 0)

    def corner_adjoint(v, _):
        vr, vc = v // 2, v % 2
        at_r = pl.multiple_of(vr * rim, 128)
        at_c = vc * rim
        flat_adjoint(5 + v, wedge[vc, pl.ds(at_r, M), :], k_rowT[v], k_sc[v], k_colT[v],
                     at_r + (1 - 2 * vr) * side, M, (at_c + (1 - 2 * vc) * side).astype(F32))
        return 0

    lax.fori_loop(0, 4, corner_adjoint, 0)


def render_and_adjoin(prm, sky_level, counts):
    _, side, _ = counts.shape
    slots = prm.shape[2]
    M, B = MARGIN, BANDS
    vm = lambda *s: pltpu.VMEM(s, BF16)
    vf = lambda *s: pltpu.VMEM(s, F32)
    scratch = [
        pltpu.VMEM(counts.shape, counts.dtype), vf(B, side, side), vm(B, side, side), vm(2, side, B * M),
        vm(side, slots), vm(B * side, slots), vm(slots, B * side), vm(side, slots), vm(slots, side),
        vm(2, M, slots), vm(2, B * M, slots), vm(2, slots, B * M), vm(2, side, slots), vm(2, slots, side),
        vm(2, side, slots), vm(2, slots, side), vm(2, B * M, slots), vm(2, slots, B * M), vm(2, slots, M),
        vm(4, M, slots), vm(4, slots, M), vm(4, B * M, slots), vm(4, slots, B * M), vm(4, slots, M),
        vf(side, side), vf(side, slots), vf(slots, side), pltpu.SemaphoreType.DMA,
    ]
    return pl.pallas_call(
        functools.partial(core, side, slots),
        out_shape=jax.ShapeDtypeStruct((9, 8, slots), F32),
        in_specs=[
            pl.BlockSpec(memory_space=pltpu.VMEM),
            pl.BlockSpec(memory_space=pltpu.SMEM),
            pl.BlockSpec(memory_space=pl.ANY),
        ],
        out_specs=pl.BlockSpec(memory_space=pltpu.VMEM),
        scratch_shapes=scratch,
        compiler_params=pltpu.CompilerParams(vmem_limit_bytes=60 * 1024 * 1024),
    )(prm, sky_level, counts)


def on_device(log_flux, position, log_width, owner_tile, sky_level, counts):
    n_ra, n_dec = lax.axis_size("ra"), lax.axis_size("dec")
    tiles = n_ra * n_dec
    cap = max(2, 2 * CAT_DEV // tiles)
    slots = tiles * cap
    here = log_flux.shape[1]
    target = owner_tile[:, 0]
    order = jnp.arange(here, dtype=jnp.int32)
    matches = (target[:, None] == target[None, :]) & (order[None, :] < order[:, None])
    rank = jnp.sum(matches.astype(jnp.int32), axis=1)
    slot = target * cap + rank
    onehot = (slot[:, None] == jnp.arange(slots, dtype=jnp.int32)[None, :]).astype(F32)
    rows = jnp.concatenate([log_flux, position, log_width[None, :], jnp.ones((1, here), F32)], axis=0)
    sorted_rows = jnp.dot(rows, onehot, precision=lax.Precision.HIGHEST)
    sorted_flux = jnp.where(sorted_rows[8:9] > 0.5, sorted_rows[:5], EMPTY)

    def around(x, fill):
        x = jnp.pad(x.reshape(-1, n_ra, n_dec, cap), ((0, 0), (1, 1), (1, 1), (0, 0)), constant_values=fill)
        return jnp.stack([x[:, 1 + i : 1 + i + n_ra, 1 + j : 1 + j + n_dec] for i, j in AROUND])

    outgoing = jnp.concatenate([around(sorted_flux, EMPTY), around(sorted_rows[5:8], 0.0)], axis=1)
    outgoing = outgoing.transpose(2, 3, 1, 0, 4).reshape(tiles, 8, 9 * cap)
    arrived = lax.all_to_all(outgoing, AXES, split_axis=0, concat_axis=0, tiled=True)
    prm = arrived.reshape(tiles, 8, 9, cap).transpose(2, 1, 0, 3).reshape(9, 8, slots)
    grads = render_and_adjoin(prm, sky_level, counts)
    leaving = grads.reshape(9, 8, tiles, cap).transpose(2, 1, 0, 3).reshape(tiles, 8, 9 * cap)
    back = lax.all_to_all(leaving, AXES, split_axis=0, concat_axis=0, tiled=True)
    back = back.reshape(n_ra, n_dec, 8, 9, cap)
    back = jnp.pad(back, ((1, 1), (1, 1), (0, 0), (0, 0), (0, 0)))
    total = sum(back[1 - i : 1 - i + n_ra, 1 - j : 1 - j + n_dec, :, n] for n, (i, j) in enumerate(AROUND))
    total = total.transpose(2, 0, 1, 3).reshape(8, slots)
    return jnp.dot(total, onehot.T, precision=lax.Precision.HIGHEST)


def solution(mesh):
    in_specs = (
        P(None, AXES),
        P(None, AXES),
        P(AXES),
        P(AXES, None),
        P("ra", "dec", None),
        P(None, "ra", "dec"),
    )
    return jax.shard_map(
        on_device, mesh=mesh, in_specs=in_specs, out_specs=P(None, AXES), check_vma=False
    )
```

```python
import functools
import math

import jax
import jax.numpy as jnp
from jax import lax
from jax.experimental import pallas as pl
from jax.experimental.pallas import tpu as pltpu
from jax.sharding import PartitionSpec as P

MARGIN = 128
CAT_DEV = 256
BANDS = 5
AXES = ("ra", "dec")
AROUND = [(0, 0), (-1, 0), (1, 0), (0, -1), (0, 1), (-1, -1), (-1, 1), (1, -1), (1, 1)]
EMPTY = -1e30
F32 = jnp.float32
BF16 = jnp.bfloat16


def dot(a, b):
    return jnp.dot(a, b, preferred_element_type=F32)


def dot_nt(a, b):
    return lax.dot_general(a, b, (((1,), (1,)), ((), ())), preferred_element_type=F32)


def sources(rows):
    flux = [jnp.exp(rows[b : b + 1]) for b in range(BANDS)]
    inverse = jnp.exp(-rows[7:8]) * (1.0 / MARGIN)
    scale = inverse * inverse * (-0.5 * math.log2(math.e))
    return flux, rows[5:6], rows[6:7], scale, inverse * (1.0 / math.sqrt(2.0 * math.pi)), inverse


def pixels(first, count):
    return lax.broadcasted_iota(jnp.int32, (count, 1), 0).astype(F32) + first


def fill_long(ref, length, first, center, scale, norm):
    step = 64

    def body(i, _):
        d = pixels(first + (i * step).astype(F32), step) - center
        ref[pl.ds(pl.multiple_of(i * step, step), step), :] = (jnp.exp2(d * (d * scale)) * norm).astype(BF16)
        return 0

    lax.fori_loop(0, length // step, body, 0)


def fill_short(ref, scaled, first, center, scale, norm, flux):
    step = 32
    peaks = [norm * f for f in flux]

    def body(i, _):
        d = pixels(first + (i * step).astype(F32), step) - center
        e = jnp.exp2(d * (d * scale))
        ref[pl.ds(pl.multiple_of(i * step, step), step), :] = (e * norm).astype(BF16)
        for b in range(BANDS):
            scaled[pl.ds(pl.multiple_of(b * MARGIN + i * step, step), step), :] = (e * peaks[b]).astype(BF16)
        return 0

    lax.fori_loop(0, MARGIN // step, body, 0)


def fold(x):
    total = x[:8]
    for i in range(8, x.shape[0], 8):
        total = total + x[i : i + 8]
    return total


def moments(total, first, center, scale):
    d = pixels(first, total.shape[0]) - center
    q = jnp.exp2(d * (d * scale)) * total
    q1 = q * d
    return fold(q), fold(q1), fold(q1 * d)


def reduce_short(buf, shape, first, center, scale, flux, width=256, step=16):
    slots = buf.shape[1]
    parts = []
    for lo in range(0, slots, width):
        lanes = slice(lo, lo + width)
        sums = None
        for r in range(0, MARGIN, step):
            p = shape[r : r + step, lanes].astype(F32)
            new = []
            total = None
            for b in range(BANDS):
                a = buf[b * MARGIN + r : b * MARGIN + r + step, lanes]
                new.append(fold(a * p))
                a = a * flux[b][:, lanes]
                total = a if total is None else total + a
            new.extend(moments(total, first + r, center[:, lanes], scale[:, lanes]))
            sums = new if sums is None else [s + v for s, v in zip(sums, new)]
        parts.append(sums)
    return [jnp.concatenate([p[m] for p in parts], axis=1) for m in range(BANDS + 3)]


def reduce_long(buf, length, first, center, scale, width=256, step=16):
    slots = buf.shape[1]
    parts = []
    for lo in range(0, slots, width):
        lanes = slice(lo, lo + width)
        sums = None
        for r in range(0, length, step):
            new = moments(buf[r : r + step, lanes], first + r, center[:, lanes], scale[:, lanes])
            sums = new if sums is None else [s + v for s, v in zip(sums, new)]
        parts.append(sums)
    return [jnp.concatenate([p[m] for p in parts], axis=1) for m in range(3)]


def slopes(m, norm, inverse):
    m = [jnp.sum(v, axis=0, keepdims=True) for v in m]
    square = inverse * inverse
    return norm * square * m[1], norm * (square * m[2] - m[0])


def core(side, prm, sky, counts_hbm, out, counts, w, wt, flat, strip, rim_sum,
         c_row, c_sc, c_col, e_short, e_sc, e_long, k_short, k_sc, k_long, big, xbuf, ybuf, sem):
    M = MARGIN
    chunks = side // M
    last = side - M
    fetch = pltpu.make_async_copy(counts_hbm, counts, sem)
    fetch.start()

    flux, rc, cc, scale, norm, inverse = sources(prm[0])
    fill_long(c_col, side, 0.5, cc, scale, norm)

    def own_fill(c, _):
        fill_short(c_row.at[c], c_sc.at[c], (c * M).astype(F32) + 0.5, rc, scale, norm, flux)
        return 0

    lax.fori_loop(0, chunks, own_fill, 0)

    def edge_at(e):
        return jnp.where(e % 2 == 0, side, -M).astype(F32) + 0.5

    def edge_fill(e, _):
        flux, rc, cc, scale, norm, inverse = sources(prm[1 + e])
        across = jnp.where(e < 2, rc, cc)
        along = jnp.where(e < 2, cc, rc)
        fill_short(e_short.at[e], e_sc.at[e], edge_at(e), across, scale, norm, flux)
        fill_long(e_long.at[e], side, 0.5, along, scale, norm)
        return 0

    lax.fori_loop(0, 4, edge_fill, 0)

    def corner_fill(k, _):
        flux, rc, cc, scale, norm, inverse = sources(prm[5 + k])
        fill_short(k_short.at[k], k_sc.at[k], edge_at(k), cc, scale, norm, flux)
        fill_long(k_long.at[k], M, edge_at(k // 2), rc, scale, norm)
        return 0

    lax.fori_loop(0, 4, corner_fill, 0)

    def rim_render(v, _):
        rim_sum[v] = dot_nt(e_long[2 + v], e_sc[2 + v])
        rim_sum[v, :M] += dot_nt(k_long[v], k_sc[v])
        rim_sum[v, last:] += dot_nt(k_long[2 + v], k_sc[2 + v])
        return 0

    lax.fori_loop(0, 2, rim_render, 0)

    fetch.wait()

    def own_render(c, _):
        big[...] = dot_nt(c_sc[c], c_col[...])

        @pl.when((c == 0) | (c == chunks - 1))
        def _():
            v = jnp.where(c == 0, 0, 1)
            big[...] += dot_nt(e_sc[v], e_long[v])

        rows = pl.ds(pl.multiple_of(c * M, M), M)
        for b in range(BANDS):
            band = slice(b * M, (b + 1) * M)
            level = sky[0, 0, b]
            seen = counts[b, rows, :].astype(F32)
            left = big[band, :M] + rim_sum[0, rows, band]
            right = big[band, last:] + rim_sum[1, rows, band]
            model = jnp.concatenate([left, big[band, M:last], right], axis=1)
            weights = (seen / (model + level) - 1.0).astype(BF16)
            turned = weights.T
            w[c, band, :] = weights
            wt[c, :, band] = turned
            flat[0, rows, band] = weights[:, :M]
            flat[1, rows, band] = weights[:, last:]
            strip[0, band, rows] = turned[:M]
            strip[1, band, rows] = turned[last:]
        return 0

    lax.fori_loop(0, chunks, own_render, 0)

    def own_adjoint(c, sums):
        xbuf[...] = dot(w[c], c_col[...])
        found = reduce_short(xbuf, c_row.at[c], (c * M).astype(F32) + 0.5, rc, scale, flux)

        @pl.when(c == 0)
        def _():
            ybuf[...] = dot(wt[c], c_sc[c])

        @pl.when(c > 0)
        def _():
            ybuf[...] += dot(wt[c], c_sc[c])

        return tuple(s + f for s, f in zip(sums, found))

    slots = prm.shape[2]
    found = lax.fori_loop(0, chunks, own_adjoint, (jnp.zeros((8, slots), F32),) * (BANDS + 3))
    nothing = jnp.zeros((1, slots), F32)
    sums = [jnp.sum(s, axis=0, keepdims=True) * f for s, f in zip(found[:BANDS], flux)]
    row_grad, width_r = slopes(found[BANDS:], norm, inverse)
    col_grad, width_c = slopes(reduce_long(ybuf, side, 0.5, cc, scale), norm, inverse)
    out[0] = jnp.concatenate(sums + [row_grad, col_grad, width_r + width_c], axis=0)

    def edge_adjoint(e, _):
        flux, rc, cc, scale, norm, inverse = sources(prm[1 + e])
        across = jnp.where(e < 2, rc, cc)
        along = jnp.where(e < 2, cc, rc)

        @pl.when(e < 2)
        def _():
            c = jnp.where(e == 0, 0, chunks - 1)
            xbuf[...] = dot(w[c], e_long[e])
            ybuf[...] = dot(wt[c], e_sc[e])

        @pl.when(e >= 2)
        def _():
            xbuf[...] = dot(strip[e - 2], e_long[e])
            ybuf[...] = dot(flat[e - 2], e_sc[e])

        found = reduce_short(xbuf, e_short.at[e], edge_at(e), across, scale, flux)
        sums = [jnp.sum(s, axis=0, keepdims=True) * f for s, f in zip(found[:BANDS], flux)]
        across_grad, width_a = slopes(found[BANDS:], norm, inverse)
        along_grad, width_b = slopes(reduce_long(ybuf, side, 0.5, along, scale), norm, inverse)
        row_grad = jnp.where(e < 2, across_grad, along_grad)
        col_grad = jnp.where(e < 2, along_grad, across_grad)
        out[1 + e] = jnp.concatenate(sums + [row_grad, col_grad, width_a + width_b], axis=0)
        return 0

    lax.fori_loop(0, 4, edge_adjoint, 0)

    def corner_adjoint(k, _):
        flux, rc, cc, scale, norm, inverse = sources(prm[5 + k])
        v = k % 2
        at = pl.multiple_of((k // 2) * last, M)
        xbuf[...] = dot(strip[v, :, pl.ds(at, M)], k_long[k])
        ybuf[:M] = dot(flat[v, pl.ds(at, M), :], k_sc[k])
        found = reduce_short(xbuf, k_short.at[k], edge_at(k), cc, scale, flux)
        sums = [jnp.sum(s, axis=0, keepdims=True) * f for s, f in zip(found[:BANDS], flux)]
        col_grad, width_c = slopes(found[BANDS:], norm, inverse)
        row_grad, width_r = slopes(reduce_long(ybuf, M, edge_at(k // 2), rc, scale), norm, inverse)
        out[5 + k] = jnp.concatenate(sums + [row_grad, col_grad, width_r + width_c], axis=0)
        return 0

    lax.fori_loop(0, 4, corner_adjoint, 0)


def render_and_adjoin(prm, sky_level, counts):
    _, side, _ = counts.shape
    slots = prm.shape[2]
    M, B = MARGIN, BANDS
    chunks = side // M
    vm = lambda *s: pltpu.VMEM(s, BF16)
    vf = lambda *s: pltpu.VMEM(s, F32)
    scratch = [
        pltpu.VMEM(counts.shape, counts.dtype),
        vm(chunks, B * M, side), vm(chunks, side, B * M), vm(2, side, B * M), vm(2, B * M, side), vf(2, side, B * M),
        vm(chunks, M, slots), vm(chunks, B * M, slots), vm(side, slots),
        vm(4, M, slots), vm(4, B * M, slots), vm(4, side, slots),
        vm(4, M, slots), vm(4, B * M, slots), vm(4, M, slots),
        vf(B * M, side), vf(B * M, slots), vf(side, slots), pltpu.SemaphoreType.DMA,
    ]
    return pl.pallas_call(
        functools.partial(core, side),
        out_shape=jax.ShapeDtypeStruct((9, 8, slots), F32),
        in_specs=[
            pl.BlockSpec(memory_space=pltpu.VMEM),
            pl.BlockSpec(memory_space=pltpu.SMEM),
            pl.BlockSpec(memory_space=pl.ANY),
        ],
        out_specs=pl.BlockSpec(memory_space=pltpu.VMEM),
        scratch_shapes=scratch,
        compiler_params=pltpu.CompilerParams(vmem_limit_bytes=60 * 1024 * 1024),
    )(prm, sky_level, counts)


def on_device(log_flux, position, log_width, owner_tile, sky_level, counts):
    n_ra, n_dec = lax.axis_size("ra"), lax.axis_size("dec")
    tiles = n_ra * n_dec
    cap = max(2, 2 * CAT_DEV // tiles)
    slots = tiles * cap
    here = log_flux.shape[1]
    target = owner_tile[:, 0]
    order = jnp.arange(here, dtype=jnp.int32)
    matches = (target[:, None] == target[None, :]) & (order[None, :] < order[:, None])
    rank = jnp.sum(matches.astype(jnp.int32), axis=1)
    slot = target * cap + rank
    onehot = (slot[:, None] == jnp.arange(slots, dtype=jnp.int32)[None, :]).astype(F32)
    rows = jnp.concatenate([log_flux, position, log_width[None, :], jnp.ones((1, here), F32)], axis=0)
    sorted_rows = jnp.dot(rows, onehot, precision=lax.Precision.HIGHEST)
    sorted_flux = jnp.where(sorted_rows[8:9] > 0.5, sorted_rows[:5], EMPTY)

    def around(x, fill):
        x = jnp.pad(x.reshape(-1, n_ra, n_dec, cap), ((0, 0), (1, 1), (1, 1), (0, 0)), constant_values=fill)
        return jnp.stack([x[:, 1 + i : 1 + i + n_ra, 1 + j : 1 + j + n_dec] for i, j in AROUND])

    outgoing = jnp.concatenate([around(sorted_flux, EMPTY), around(sorted_rows[5:8], 0.0)], axis=1)
    outgoing = outgoing.transpose(2, 3, 1, 0, 4).reshape(tiles, 8, 9 * cap)
    arrived = lax.all_to_all(outgoing, AXES, split_axis=0, concat_axis=0, tiled=True)
    prm = arrived.reshape(tiles, 8, 9, cap).transpose(2, 1, 0, 3).reshape(9, 8, slots)
    grads = render_and_adjoin(prm, sky_level, counts)
    leaving = grads.reshape(9, 8, tiles, cap).transpose(2, 1, 0, 3).reshape(tiles, 8, 9 * cap)
    back = lax.all_to_all(leaving, AXES, split_axis=0, concat_axis=0, tiled=True)
    back = back.reshape(n_ra, n_dec, 8, 9, cap)
    back = jnp.pad(back, ((1, 1), (1, 1), (0, 0), (0, 0), (0, 0)))
    total = sum(back[1 - i : 1 - i + n_ra, 1 - j : 1 - j + n_dec, :, n] for n, (i, j) in enumerate(AROUND))
    total = total.transpose(2, 0, 1, 3).reshape(8, slots)
    return jnp.dot(total, onehot.T, precision=lax.Precision.HIGHEST)


def solution(mesh):
    in_specs = (
        P(None, AXES),
        P(None, AXES),
        P(AXES),
        P(AXES, None),
        P("ra", "dec", None),
        P(None, "ra", "dec"),
    )
    return jax.shard_map(
        on_device, mesh=mesh, in_specs=in_specs, out_specs=P(None, AXES), check_vma=False
    )
```

```python
import functools
import math

import jax
import jax.numpy as jnp
from jax import lax
from jax.experimental import pallas as pl
from jax.experimental.pallas import tpu as pltpu
from jax.sharding import PartitionSpec as P

MARGIN = 128
CAT_DEV = 256
BANDS = 5
AXES = ("ra", "dec")
AROUND = [(0, 0), (-1, 0), (1, 0), (0, -1), (0, 1), (-1, -1), (-1, 1), (1, -1), (1, 1)]
EMPTY = -1e30
F32 = jnp.float32
BF16 = jnp.bfloat16


def dot(a, b):
    return jnp.dot(a, b, preferred_element_type=F32)


def dot_nt(a, b):
    return lax.dot_general(a, b, (((1,), (1,)), ((), ())), preferred_element_type=F32)


def dot_tn(a, b):
    return lax.dot_general(a, b, (((0,), (0,)), ((), ())), preferred_element_type=F32)


def sources(rows):
    flux = [jnp.exp(rows[b : b + 1]) for b in range(BANDS)]
    inverse = jnp.exp(-rows[7:8]) * (1.0 / MARGIN)
    scale = inverse * inverse * (-0.5 * math.log2(math.e))
    return flux, rows[5:6], rows[6:7], scale, inverse * (1.0 / math.sqrt(2.0 * math.pi)), inverse


def distance(first, count, center):
    return lax.broadcasted_iota(jnp.int32, (count, 1), 0).astype(F32) + first - center


def fill_long(ref, length, first, center, scale, norm, step=32, width=128):
    for lo in range(0, ref.shape[1], width):
        lanes = slice(lo, lo + width)
        d0 = distance(first, step, center[:, lanes])
        for r in range(0, length, step):
            d = d0 + float(r)
            ref[r : r + step, lanes] = (jnp.exp2(d * (d * scale[:, lanes])) * norm[:, lanes]).astype(BF16)


def fill_scaled(ref, first, center, scale, norm, flux, step=32, width=128):
    for lo in range(0, ref.shape[1], width):
        lanes = slice(lo, lo + width)
        d0 = distance(first, step, center[:, lanes])
        peaks = [norm[:, lanes] * f[:, lanes] for f in flux]
        for r in range(0, MARGIN, step):
            d = d0 + float(r)
            e = jnp.exp2(d * (d * scale[:, lanes]))
            for b in range(BANDS):
                ref[b * MARGIN + r : b * MARGIN + r + step, lanes] = (e * peaks[b]).astype(BF16)


def fold(x):
    total = x[:8]
    for i in range(8, x.shape[0], 8):
        total = total + x[i : i + 8]
    return total


def reduce_short(buf, first, center, scale, flux, step=32, width=128):
    parts = []
    for lo in range(0, buf.shape[1], width):
        lanes = slice(lo, lo + width)
        fluxes = [f[:, lanes] for f in flux]
        d0 = distance(first, step, center[:, lanes])
        sums = None
        for r in range(0, MARGIN, step):
            d = d0 + float(r)
            e = jnp.exp2(d * (d * scale[:, lanes]))
            new = []
            total = None
            for b in range(BANDS):
                a = buf[b * MARGIN + r : b * MARGIN + r + step, lanes] * e
                new.append(fold(a))
                a = a * fluxes[b]
                total = a if total is None else total + a
            q = total * d
            new.extend([fold(q), fold(q * d)])
            sums = new if sums is None else [s + v for s, v in zip(sums, new)]
        parts.append(sums)
    found = [jnp.concatenate([p[m] for p in parts], axis=1) for m in range(BANDS + 2)]
    return [found[m] * flux[m] for m in range(BANDS)] + found[BANDS:]


def reduce_long(buf, length, first, center, scale, step=32, width=128):
    parts = []
    for lo in range(0, buf.shape[1], width):
        lanes = slice(lo, lo + width)
        d0 = distance(first, step, center[:, lanes])
        sums = None
        for r in range(0, length, step):
            d = d0 + float(r)
            q = jnp.exp2(d * (d * scale[:, lanes])) * buf[r : r + step, lanes]
            q1 = q * d
            new = [fold(q), fold(q1), fold(q1 * d)]
            sums = new if sums is None else [s + v for s, v in zip(sums, new)]
        parts.append(sums)
    return [jnp.concatenate([p[m] for p in parts], axis=1) for m in range(3)]


def settle(short, long, norm, inverse):
    short = [jnp.sum(v, axis=0, keepdims=True) * norm for v in short]
    long = [jnp.sum(v, axis=0, keepdims=True) * norm for v in long]
    square = inverse * inverse
    bands = short[:BANDS]
    zeroth = bands[0] + bands[1] + bands[2] + bands[3] + bands[4]
    width = square * short[BANDS + 1] - zeroth + (square * long[2] - long[0])
    return bands, square * short[BANDS], square * long[1], width


def core(side, cap, arrived, sky, counts_hbm, leaving, prm, out, counts, canvas, w, w_next, side_w, rim_sum,
         c_sc, c_col, e_sc, e_long, k_sc, k_long, xa, xb, yb, yk, sem):
    M = MARGIN
    chunks = side // M
    last = side - M
    fetch = pltpu.make_async_copy(counts_hbm, counts, sem)
    fetch.start()
    tiles = arrived.shape[0] // 9
    slots = prm.shape[2]
    for n in range(9):
        table = arrived[pl.ds(n, tiles, stride=9), :].T
        prm[n] = jnp.concatenate([table[8 * r : 8 * r + 8] for r in range(cap)], axis=1)

    def number(c):
        return c.astype(F32) * float(M) + 0.5

    flux, rc, cc, scale, norm, inverse = sources(prm[0])

    def col_fill(c, _):
        at = pl.multiple_of(c * M, M)
        fill_long(c_col.at[pl.ds(at, M), :], M, number(c), cc, scale, norm)
        fill_scaled(c_sc.at[c], number(c), rc, scale, norm, flux)
        return 0

    lax.fori_loop(0, chunks, col_fill, 0)

    def edge_fill(e, across_is_row, at, index):
        flux, rc, cc, scale, norm, _ = sources(prm[index])
        across = jnp.where(across_is_row, rc, cc)
        along = jnp.where(across_is_row, cc, rc)
        fill_scaled(e_sc.at[e], at, across, scale, norm, flux)
        fill_long(e_long.at[e], side, 0.5, along, scale, norm)

    def corner_fill(k, left, v):
        flux, rc, cc, scale, norm, _ = sources(prm[5 + k])
        fill_scaled(k_sc.at[k], (side if left else -M) + 0.5, cc, scale, norm, flux)
        fill_long(k_long.at[k], M, jnp.where(v == 0, side, -M).astype(F32) + 0.5, rc, scale, norm)

    def own_render(c, _):
        canvas[c] = dot_nt(c_sc[c], c_col[...])
        edge_fill(c, c < 2, jnp.where(c % 2 == 0, side, -M).astype(F32) + 0.5, 1 + c)
        return 0

    lax.fori_loop(0, 4, own_render, 0)

    def more_render(c, _):
        canvas[c] = dot_nt(c_sc[c], c_col[...])
        return 0

    lax.fori_loop(4, chunks, more_render, 0)

    def rim_render(v, _):
        rim_sum[v] = dot_nt(e_long[2 + v], e_sc[2 + v])
        corner_fill(2 * v, True, v)
        corner_fill(2 * v + 1, False, v)
        return 0

    lax.fori_loop(0, 2, rim_render, 0)

    fetch.wait()

    def weigh(c, own):
        rows = pl.ds(pl.multiple_of(c * M, M), M)
        for b in range(BANDS):
            band = slice(b * M, (b + 1) * M)
            level = sky[0, 0, b]
            seen = counts[b, rows, :].astype(F32)
            left = canvas[c, band, :M] + rim_sum[0, rows, band]
            right = canvas[c, band, last:] + rim_sum[1, rows, band]
            model = jnp.concatenate([left, canvas[c, band, M:last], right], axis=1)
            weights = (seen / (model + level) - 1.0).astype(BF16)
            own[band, :] = weights
            side_w[0, band, rows] = weights[:, :M].T
            side_w[1, band, rows] = weights[:, last:].T

    def end_render(v, _):
        at = pl.ds(pl.multiple_of(v * last, M), M)
        rim_sum[0, at] += dot_nt(k_long[2 * v], k_sc[2 * v])
        rim_sum[1, at] += dot_nt(k_long[2 * v + 1], k_sc[2 * v + 1])
        canvas[v * (chunks - 1)] += dot_nt(e_sc[v], e_long[v])
        return 0

    lax.fori_loop(0, 2, end_render, 0)
    weigh(jnp.int32(0), w.at[0])

    yb[...] = jnp.zeros_like(yb)

    def own_adjoint(c, sums):
        xa[...] = dot(w[c], c_col[...])
        yb[...] += dot_tn(w[c], c_sc[c])
        later = jnp.minimum(c + 1, chunks - 1)
        weigh(later, w_next)
        found = reduce_short(xa, number(c), rc, scale, flux)
        w[later] = w_next[...]
        return tuple(s + f for s, f in zip(sums, found))

    short = lax.fori_loop(0, chunks, own_adjoint, (jnp.zeros((8, slots), F32),) * (BANDS + 2))
    w[chunks] = side_w[0]
    w[chunks + 1] = side_w[1]

    def settle_tile(g, short):
        _, rc, cc, scale, norm, inverse = sources(prm[g])
        rows_short = g < 3
        long = reduce_long(yb, side, 0.5, jnp.where(rows_short, cc, rc), scale)
        bands, across, along, width = settle(short, long, norm, inverse)
        row_grad = jnp.where(rows_short, across, along)
        col_grad = jnp.where(rows_short, along, across)
        out[g] = jnp.concatenate(bands + [row_grad, col_grad, width], axis=0)

    def settle_corner(k):
        flux, rc, cc, scale, norm, inverse = sources(prm[5 + k])
        found = reduce_short(xb, jnp.where(k % 2 == 0, side, -M).astype(F32) + 0.5, cc, scale, flux)
        long = reduce_long(yk, M, jnp.where(k < 2, side, -M).astype(F32) + 0.5, rc, scale)
        bands, col_grad, row_grad, width = settle(found, long, norm, inverse)
        out[5 + k] = jnp.concatenate(bands + [row_grad, col_grad, width], axis=0)

    def edge_adjoint(e, short):
        settle_corner(e - 1)
        settle_tile(e, short)
        v, at = e % 2, pl.ds(pl.multiple_of(e // 2 * last, M), M)
        strip = jnp.where(e == 0, 0, e + chunks - 2)
        xa[...] = dot(w[strip], e_long[e])
        xb[...] = dot(w[chunks + v, :, at], k_long[e])
        yk[...] = dot_tn(w[chunks + v, :, at], k_sc[e])
        yb[...] = dot_tn(w[strip], e_sc[e])
        flux, rc, cc, scale, _, _ = sources(prm[1 + e])
        first = jnp.where(v == 0, side, -M).astype(F32) + 0.5
        return tuple(reduce_short(xa, first, jnp.where(e < 2, rc, cc), scale, flux))

    short = lax.fori_loop(0, 4, edge_adjoint, tuple(short))
    settle_corner(jnp.int32(3))
    settle_tile(4, short)

    for n in range(9):
        found = out[n]
        rows = [found[:, r * tiles : (r + 1) * tiles] for r in range(cap)]
        if cap < 16:
            rows.append(jnp.zeros((128 - 8 * cap, tiles), F32))
        leaving[pl.ds(n, tiles, stride=9), :] = jnp.concatenate(rows, axis=0).T


def render_and_adjoin(arrived, sky_level, counts, cap):
    _, side, _ = counts.shape
    slots = arrived.shape[0] // 9 * cap
    M, B = MARGIN, BANDS
    chunks = side // M
    vm = lambda *s: pltpu.VMEM(s, BF16)
    vf = lambda *s: pltpu.VMEM(s, F32)
    scratch = [
        vf(9, 8, slots), vf(9, 8, slots), pltpu.VMEM(counts.shape, counts.dtype), vf(chunks, B * M, side),
        vm(chunks + 2, B * M, side), vm(B * M, side), vm(2, B * M, side), vf(2, side, B * M),
        vm(chunks, B * M, slots), vm(side, slots),
        vm(4, B * M, slots), vm(4, side, slots),
        vm(4, B * M, slots), vm(4, M, slots),
        vf(B * M, slots), vf(B * M, slots), vf(side, slots), vf(M, slots),
        pltpu.SemaphoreType.DMA,
    ]
    return pl.pallas_call(
        functools.partial(core, side, cap),
        out_shape=jax.ShapeDtypeStruct(arrived.shape, F32),
        in_specs=[
            pl.BlockSpec(memory_space=pltpu.VMEM),
            pl.BlockSpec(memory_space=pltpu.SMEM),
            pl.BlockSpec(memory_space=pl.ANY),
        ],
        out_specs=pl.BlockSpec(memory_space=pltpu.VMEM),
        scratch_shapes=scratch,
        compiler_params=pltpu.CompilerParams(vmem_limit_bytes=60 * 1024 * 1024),
    )(arrived, sky_level, counts)


def exact_dot(hot, values, contract):
    high = values.astype(BF16)
    rest = values - high.astype(F32)
    middle = rest.astype(BF16)
    low = (rest - middle.astype(F32)).astype(BF16)
    total = None
    for part in (low, middle, high):
        found = lax.dot_general(hot, part, (contract, ((), ())), preferred_element_type=F32)
        total = found if total is None else total + found
    return total


def ranks(owner_row):
    here = owner_row.shape[1]
    first = lax.broadcasted_iota(jnp.int32, (here, here), 0)
    second = lax.broadcasted_iota(jnp.int32, (here, here), 1)
    numbers = owner_row.astype(F32)
    column = jnp.broadcast_to(numbers, (8, here)).T[:, :1]
    same = (column == numbers) & (first < second)
    return jnp.sum(jnp.where(same, 1.0, 0.0), axis=0, keepdims=True).astype(jnp.int32)


def turned(x, shift):
    shift = shift % x.shape[0]
    return x if shift == 0 else jnp.concatenate([x[shift:], x[:shift]], axis=0)


def send_rows(n_ra, n_dec, cap, log_flux, position, log_width, owner, out):
    tiles = n_ra * n_dec
    here = owner.shape[1]
    owner_row = owner[...]
    rank_row = ranks(owner_row)
    rows = jnp.concatenate([log_flux[...], position[...], log_width[...]], axis=0)
    place = lax.broadcasted_iota(jnp.int32, (128, here), 0)
    mine = (place // 8 == rank_row) & (rank_row < cap)
    spread = jnp.where(mine, jnp.concatenate([rows] * 16, axis=0), 0.0)
    hot = (lax.broadcasted_iota(jnp.int32, (tiles, here), 0) == owner_row).astype(F32).astype(BF16)
    contract = ((1,), (1,))
    base = exact_dot(hot, spread, contract)
    taken = lax.dot_general(hot, mine.astype(F32).astype(BF16), (contract, ((), ())), preferred_element_type=F32)
    lane = lax.broadcasted_iota(jnp.int32, (tiles, 128), 1) % 8
    empty = jnp.where(lane < BANDS, EMPTY, 0.0)
    base = jnp.where(taken > 0.5, base, empty)
    tile = lax.broadcasted_iota(jnp.int32, (tiles, 1), 0)
    at_ra, at_dec = tile // n_dec, tile % n_dec
    for n, (i, j) in enumerate(AROUND):
        inside = (at_ra + i >= 0) & (at_ra + i < n_ra) & (at_dec + j >= 0) & (at_dec + j < n_dec)
        out[pl.ds(n, tiles, stride=9), :] = jnp.where(inside, turned(base, i * n_dec + j), empty)


def collect_rows(n_ra, n_dec, cap, arrived, owner, out):
    tiles = n_ra * n_dec
    here = owner.shape[1]
    owner_row = owner[...]
    rank_row = ranks(owner_row)
    total = None
    for n, (i, j) in enumerate(AROUND):
        part = turned(arrived[pl.ds(n, tiles, stride=9), :], -(i * n_dec + j))
        total = part if total is None else total + part
    hot = (lax.broadcasted_iota(jnp.int32, (tiles, here), 0) == owner_row).astype(F32).astype(BF16)
    picked = exact_dot(hot, total, ((0,), (0,))).T
    place = lax.broadcasted_iota(jnp.int32, (128, here), 0) // 8
    picked = jnp.where(place == rank_row, picked, 0.0)
    found = picked[:8]
    for r in range(1, cap):
        found = found + picked[8 * r : 8 * r + 8]
    out[...] = found


def on_device(log_flux, position, log_width, owner_tile, sky_level, counts):
    n_ra, n_dec = lax.axis_size("ra"), lax.axis_size("dec")
    tiles = n_ra * n_dec
    cap = max(2, 2 * CAT_DEV // tiles)
    here = log_flux.shape[1]
    owner = owner_tile.reshape(1, here)
    box = jax.ShapeDtypeStruct((9 * tiles, 128), F32)
    leaving = pl.pallas_call(functools.partial(send_rows, n_ra, n_dec, cap), out_shape=box)(
        log_flux, position, log_width[None, :], owner
    )
    arrived = lax.all_to_all(leaving.reshape(-1), AXES, split_axis=0, concat_axis=0, tiled=True)
    partial = render_and_adjoin(arrived.reshape(box.shape), sky_level, counts, cap)
    back = lax.all_to_all(partial.reshape(-1), AXES, split_axis=0, concat_axis=0, tiled=True)
    return pl.pallas_call(
        functools.partial(collect_rows, n_ra, n_dec, cap), out_shape=jax.ShapeDtypeStruct((8, here), F32)
    )(back.reshape(box.shape), owner)


def solution(mesh):
    in_specs = (
        P(None, AXES),
        P(None, AXES),
        P(AXES),
        P(AXES, None),
        P("ra", "dec", None),
        P(None, "ra", "dec"),
    )
    return jax.shard_map(
        on_device, mesh=mesh, in_specs=in_specs, out_specs=P(None, AXES), check_vma=False
    )
```

```python
import functools
import math

import jax
import jax.numpy as jnp
from jax import lax
from jax.experimental import pallas as pl
from jax.experimental.pallas import tpu as pltpu
from jax.sharding import PartitionSpec as P

MARGIN = 128
CAT_DEV = 256
BANDS = 5
AXES = ("ra", "dec")
AROUND = [(0, 0), (-1, 0), (1, 0), (0, -1), (0, 1), (-1, -1), (-1, 1), (1, -1), (1, 1)]
EMPTY = -1e30
F32 = jnp.float32
BF16 = jnp.bfloat16


def dot(a, b):
    return jnp.dot(a, b, preferred_element_type=F32)


def dot_nt(a, b):
    return lax.dot_general(a, b, (((1,), (1,)), ((), ())), preferred_element_type=F32)


def dot_tn(a, b):
    return lax.dot_general(a, b, (((0,), (0,)), ((), ())), preferred_element_type=F32)


ROW, COL, INVERSE, SCALE, PEAK, PEAKS = 5, 6, 7, 8, 9, 16


def derive(table, rows):
    index = lax.broadcasted_iota(jnp.int32, rows.shape, 0)
    powers = jnp.exp(jnp.where(index < BANDS, rows, jnp.where(index == 7, -rows, 0.0)))
    inverse = powers[7:8] * (1.0 / MARGIN)
    peak = inverse * (1.0 / math.sqrt(2.0 * math.pi))
    table[:7] = jnp.where(index < BANDS, powers, rows)[:7]
    table[INVERSE : INVERSE + 1] = inverse
    table[SCALE : SCALE + 1] = inverse * inverse * (-0.5 * math.log2(math.e))
    table[PEAK : PEAK + 1] = peak
    table[PEAKS : PEAKS + 8] = powers * peak


def row(table, i, lanes=slice(None)):
    if isinstance(i, int):
        return table[i : i + 1, lanes]
    return jnp.where(i == ROW, table[ROW : ROW + 1, lanes], table[COL : COL + 1, lanes])


def distance(first, count, center):
    return lax.broadcasted_iota(jnp.int32, (count, 1), 0).astype(F32) + first - center


def fill_long(ref, full, length, first, table, axis, step=32, width=128):
    for lo in range(0, ref.shape[1], width):
        lanes = slice(lo, lo + width)
        d0 = distance(first, step, row(table, axis, lanes))
        scale, peak = row(table, SCALE, lanes), row(table, PEAK, lanes)
        for r in range(0, length, step):
            d = d0 + float(r)
            p = jnp.exp2(d * (d * scale)) * peak
            full[r : r + step, lanes] = p
            ref[r : r + step, lanes] = p.astype(BF16)


def fill_scaled(ref, first, table, axis, step=32, width=128):
    for lo in range(0, ref.shape[1], width):
        lanes = slice(lo, lo + width)
        d0 = distance(first, step, row(table, axis, lanes))
        scale = row(table, SCALE, lanes)
        peaks = [row(table, PEAKS + b, lanes) for b in range(BANDS)]
        for r in range(0, MARGIN, step):
            d = d0 + float(r)
            e = jnp.exp2(d * (d * scale))
            for b in range(BANDS):
                ref[b * MARGIN + r : b * MARGIN + r + step, lanes] = (e * peaks[b]).astype(BF16)


def fold(x):
    total = x[:8]
    for i in range(8, x.shape[0], 8):
        total = total + x[i : i + 8]
    return total


def reduce_short(buf, first, table, axis, step=32, width=128):
    parts = []
    for lo in range(0, buf.shape[1], width):
        lanes = slice(lo, lo + width)
        fluxes = [row(table, b, lanes) for b in range(BANDS)]
        scale = row(table, SCALE, lanes)
        d0 = distance(first, step, row(table, axis, lanes))
        sums = None
        for r in range(0, MARGIN, step):
            d = d0 + float(r)
            e = jnp.exp2(d * (d * scale))
            new = []
            total = None
            for b in range(BANDS):
                a = buf[b * MARGIN + r : b * MARGIN + r + step, lanes] * e
                new.append(fold(a))
                a = a * fluxes[b]
                total = a if total is None else total + a
            q = total * d
            new.extend([fold(q), fold(q * d)])
            sums = new if sums is None else [s + v for s, v in zip(sums, new)]
        parts.append([s * f for s, f in zip(sums, fluxes)] + sums[BANDS:])
    return [jnp.concatenate([p[m] for p in parts], axis=1) for m in range(BANDS + 2)]


def reduce_long(buf, shape, length, first, table, axis, step=32, width=128):
    parts = []
    for lo in range(0, buf.shape[1], width):
        lanes = slice(lo, lo + width)
        d0 = distance(first, step, row(table, axis, lanes))
        sums = None
        for r in range(0, length, step):
            q = shape[r : r + step, lanes] * buf[r : r + step, lanes]
            d = d0 + float(r)
            q1 = q * d
            new = [fold(q), fold(q1), fold(q1 * d)]
            sums = new if sums is None else [s + v for s, v in zip(sums, new)]
        parts.append(sums)
    return [jnp.concatenate([p[m] for p in parts], axis=1) for m in range(3)]


def settle(short, long, table):
    peak, inverse = row(table, PEAK), row(table, INVERSE)
    short = [jnp.sum(v, axis=0, keepdims=True) * peak for v in short]
    long = [jnp.sum(v, axis=0, keepdims=True) for v in long]
    square = inverse * inverse
    bands = short[:BANDS]
    zeroth = bands[0] + bands[1] + bands[2] + bands[3] + bands[4]
    width = square * short[BANDS + 1] - zeroth + (square * long[2] - long[0])
    return bands, square * short[BANDS], square * long[1], width


def core(side, cap, arrived, sky, counts_hbm, leaving, prm, out, counts, canvas, w, rim_sum,
         c_sc, e_sc, e_long, k_sc, k_long, xa, xb, yb, yk, e_full, k_full, sem):
    M = MARGIN
    chunks = side // M
    last = side - M
    fetch = pltpu.make_async_copy(counts_hbm, counts, sem)
    fetch.start()
    tiles = arrived.shape[0] // 9
    slots = prm.shape[2]
    for n in range(9):
        table = arrived[pl.ds(n, tiles, stride=9), :].T
        derive(prm.at[n], jnp.concatenate([table[8 * r : 8 * r + 8] for r in range(cap)], axis=1))

    def number(c):
        return c.astype(F32) * float(M) + 0.5

    def rim_at(i):
        return side if i % 2 == 0 else -M

    own = prm.at[0]

    def own_fill(c, _):
        at = pl.multiple_of(c * M, M)
        fill_long(e_long.at[0, pl.ds(at, M), :], e_full.at[0, pl.ds(at, M), :], M, number(c), own, COL)
        fill_scaled(c_sc.at[c], number(c), own, ROW)
        return 0

    lax.fori_loop(0, chunks, own_fill, 0)

    for c in range(chunks):
        canvas[c] = dot_nt(c_sc[c], e_long[0])
        if c < 4:
            across, along = (ROW, COL) if c < 2 else (COL, ROW)
            fill_scaled(e_sc.at[c], (side if c % 2 == 0 else -M) + 0.5, prm.at[1 + c], across)
            fill_long(e_long.at[1 + c], e_full.at[1 + c], side, 0.5, prm.at[1 + c], along)
            fill_scaled(k_sc.at[c], (side if c % 2 == 0 else -M) + 0.5, prm.at[5 + c], COL)
            fill_long(k_long.at[c], k_full.at[c], M, (side if c < 2 else -M) + 0.5, prm.at[5 + c], ROW)

    def rim_render(v, _):
        rim_sum[v] = dot_nt(e_long[3 + v], e_sc[2 + v])
        canvas[v * (chunks - 1)] += dot_nt(e_sc[v], e_long[1 + v])
        rim_sum[v, :M] += dot_nt(k_long[v], k_sc[v])
        rim_sum[v, last:] += dot_nt(k_long[2 + v], k_sc[2 + v])
        return 0

    for v in range(2):
        rim_render(v, 0)

    fetch.wait()

    def weigh(c, own):
        rows = slice(c * M, c * M + M)
        for b in range(BANDS):
            band = slice(b * M, (b + 1) * M)
            level = sky[0, 0, b]
            seen = counts[b, rows, :].astype(F32)
            left = canvas[c, band, :M] + rim_sum[0, rows, band]
            right = canvas[c, band, last:] + rim_sum[1, rows, band]
            model = jnp.concatenate([left, canvas[c, band, M:last], right], axis=1)
            weights = (seen / (model + level) - 1.0).astype(BF16)
            own[band, :] = weights
            w[chunks, band, rows] = weights[:, :M].T
            w[chunks + 1, band, rows] = weights[:, last:].T

    weigh(0, w.at[0])

    own_short = None
    for c in range(chunks):
        if c > 0:
            found = reduce_short(xa, (c - 1) * M + 0.5, own, ROW)
            own_short = found if own_short is None else [s + f for s, f in zip(own_short, found)]
        xa[...] = dot(w[c], e_long[0])
        part = dot_tn(w[c], c_sc[c])
        yb[...] = part if c == 0 else yb[...] + part
        if c < chunks - 1:
            weigh(c + 1, w.at[c + 1])

    def settle_tile(g):
        table = prm.at[g]
        short_axis, long_axis = (ROW, COL) if g < 3 else (COL, ROW)
        first = (last if g == 0 else rim_at(g - 1)) + 0.5
        short = reduce_short(xa, first, table, short_axis)
        if g == 0:
            short = [s + h for s, h in zip(short, own_short)]
        long = reduce_long(yb, e_full.at[g], side, 0.5, table, long_axis)
        bands, across, along, width = settle(short, long, table)
        grads = [across, along] if g < 3 else [along, across]
        out[g] = jnp.concatenate(bands + grads + [width], axis=0)

    def settle_corner(k):
        table = prm.at[5 + k]
        found = reduce_short(xb, rim_at(k) + 0.5, table, COL)
        long = reduce_long(yk, k_full.at[k], M, rim_at(k // 2) + 0.5, table, ROW)
        bands, col_grad, row_grad, width = settle(found, long, table)
        out[5 + k] = jnp.concatenate(bands + [row_grad, col_grad, width], axis=0)

    for e in range(4):
        settle_tile(e)
        if e > 0:
            settle_corner(e - 1)
        strip = (0, chunks - 1, chunks, chunks + 1)[e]
        rim, at = chunks + e % 2, slice(e // 2 * last, e // 2 * last + M)
        xa[...] = dot(w[strip], e_long[1 + e])
        xb[...] = dot(w[rim, :, at], k_long[e])
        yk[...] = dot_tn(w[rim, :, at], k_sc[e])
        yb[...] = dot_tn(w[strip], e_sc[e])
    settle_corner(3)
    settle_tile(4)

    for n in range(9):
        found = out[n]
        rows = [found[:, r * tiles : (r + 1) * tiles] for r in range(cap)]
        if cap < 16:
            rows.append(jnp.zeros((128 - 8 * cap, tiles), F32))
        leaving[pl.ds(n, tiles, stride=9), :] = jnp.concatenate(rows, axis=0).T


def render_and_adjoin(arrived, sky_level, counts, cap):
    _, side, _ = counts.shape
    slots = arrived.shape[0] // 9 * cap
    M, B = MARGIN, BANDS
    chunks = side // M
    vm = lambda *s: pltpu.VMEM(s, BF16)
    vf = lambda *s: pltpu.VMEM(s, F32)
    scratch = [
        vf(9, 24, slots), vf(9, 8, slots), pltpu.VMEM(counts.shape, counts.dtype), vf(chunks, B * M, side),
        vm(chunks + 2, B * M, side), vf(2, side, B * M),
        vm(chunks, B * M, slots),
        vm(4, B * M, slots), vm(5, side, slots),
        vm(4, B * M, slots), vm(4, M, slots),
        vf(B * M, slots), vf(B * M, slots), vf(side, slots), vf(M, slots),
        vf(5, side, slots), vf(4, M, slots),
        pltpu.SemaphoreType.DMA,
    ]
    return pl.pallas_call(
        functools.partial(core, side, cap),
        out_shape=jax.ShapeDtypeStruct(arrived.shape, F32),
        in_specs=[
            pl.BlockSpec(memory_space=pltpu.VMEM),
            pl.BlockSpec(memory_space=pltpu.SMEM),
            pl.BlockSpec(memory_space=pl.ANY),
        ],
        out_specs=pl.BlockSpec(memory_space=pltpu.VMEM),
        scratch_shapes=scratch,
        compiler_params=pltpu.CompilerParams(vmem_limit_bytes=60 * 1024 * 1024),
    )(arrived, sky_level, counts)


def exact_dot(hot, values, contract):
    high = values.astype(BF16)
    rest = values - high.astype(F32)
    middle = rest.astype(BF16)
    low = (rest - middle.astype(F32)).astype(BF16)
    total = None
    for part in (low, middle, high):
        found = lax.dot_general(hot, part, (contract, ((), ())), preferred_element_type=F32)
        total = found if total is None else total + found
    return total


def ranks(owner_row):
    here = owner_row.shape[1]
    first = lax.broadcasted_iota(jnp.int32, (here, here), 0)
    second = lax.broadcasted_iota(jnp.int32, (here, here), 1)
    numbers = owner_row.astype(F32)
    column = jnp.broadcast_to(numbers, (8, here)).T[:, :1]
    same = (column == numbers) & (first < second)
    return jnp.sum(jnp.where(same, 1.0, 0.0), axis=0, keepdims=True).astype(jnp.int32)


def turned(x, shift):
    shift = shift % x.shape[0]
    return x if shift == 0 else jnp.concatenate([x[shift:], x[:shift]], axis=0)


def send_rows(n_ra, n_dec, cap, log_flux, position, log_width, owner, out):
    tiles = n_ra * n_dec
    here = owner.shape[1]
    owner_row = owner[...]
    rank_row = ranks(owner_row)
    rows = jnp.concatenate([log_flux[...], position[...], log_width[...]], axis=0)
    place = lax.broadcasted_iota(jnp.int32, (128, here), 0)
    mine = (place // 8 == rank_row) & (rank_row < cap)
    spread = jnp.where(mine, jnp.concatenate([rows] * 16, axis=0), 0.0)
    hot = (lax.broadcasted_iota(jnp.int32, (tiles, here), 0) == owner_row).astype(F32).astype(BF16)
    contract = ((1,), (1,))
    base = exact_dot(hot, spread, contract)
    taken = lax.dot_general(hot, mine.astype(F32).astype(BF16), (contract, ((), ())), preferred_element_type=F32)
    lane = lax.broadcasted_iota(jnp.int32, (tiles, 128), 1) % 8
    empty = jnp.where(lane < BANDS, EMPTY, 0.0)
    base = jnp.where(taken > 0.5, base, empty)
    tile = lax.broadcasted_iota(jnp.int32, (tiles, 1), 0)
    at_ra, at_dec = tile // n_dec, tile % n_dec
    for n, (i, j) in enumerate(AROUND):
        inside = (at_ra + i >= 0) & (at_ra + i < n_ra) & (at_dec + j >= 0) & (at_dec + j < n_dec)
        out[pl.ds(n, tiles, stride=9), :] = jnp.where(inside, turned(base, i * n_dec + j), empty)


def collect_rows(n_ra, n_dec, cap, arrived, owner, out):
    tiles = n_ra * n_dec
    here = owner.shape[1]
    owner_row = owner[...]
    rank_row = ranks(owner_row)
    total = None
    for n, (i, j) in enumerate(AROUND):
        part = turned(arrived[pl.ds(n, tiles, stride=9), :], -(i * n_dec + j))
        total = part if total is None else total + part
    hot = (lax.broadcasted_iota(jnp.int32, (tiles, here), 0) == owner_row).astype(F32).astype(BF16)
    picked = exact_dot(hot, total, ((0,), (0,))).T
    place = lax.broadcasted_iota(jnp.int32, (128, here), 0) // 8
    picked = jnp.where(place == rank_row, picked, 0.0)
    found = picked[:8]
    for r in range(1, cap):
        found = found + picked[8 * r : 8 * r + 8]
    out[...] = found


def on_device(log_flux, position, log_width, owner_tile, sky_level, counts):
    n_ra, n_dec = lax.axis_size("ra"), lax.axis_size("dec")
    tiles = n_ra * n_dec
    cap = max(2, 2 * CAT_DEV // tiles)
    here = log_flux.shape[1]
    owner = owner_tile.reshape(1, here)
    box = jax.ShapeDtypeStruct((9 * tiles, 128), F32)
    leaving = pl.pallas_call(functools.partial(send_rows, n_ra, n_dec, cap), out_shape=box)(
        log_flux, position, log_width[None, :], owner
    )
    arrived = lax.all_to_all(leaving.reshape(-1), AXES, split_axis=0, concat_axis=0, tiled=True)
    partial = render_and_adjoin(arrived.reshape(box.shape), sky_level, counts, cap)
    back = lax.all_to_all(partial.reshape(-1), AXES, split_axis=0, concat_axis=0, tiled=True)
    return pl.pallas_call(
        functools.partial(collect_rows, n_ra, n_dec, cap), out_shape=jax.ShapeDtypeStruct((8, here), F32)
    )(back.reshape(box.shape), owner)


def solution(mesh):
    in_specs = (
        P(None, AXES),
        P(None, AXES),
        P(AXES),
        P(AXES, None),
        P("ra", "dec", None),
        P(None, "ra", "dec"),
    )
    return jax.shard_map(
        on_device, mesh=mesh, in_specs=in_specs, out_specs=P(None, AXES), check_vma=False
    )
```

```python
import functools
import math

import jax
import jax.numpy as jnp
from jax import lax
from jax.experimental import pallas as pl
from jax.experimental.pallas import tpu as pltpu
from jax.sharding import PartitionSpec as P

MARGIN = 128
CAT_DEV = 256
BANDS = 5
AXES = ("ra", "dec")
AROUND = [(0, 0), (-1, 0), (1, 0), (0, -1), (0, 1), (-1, -1), (-1, 1), (1, -1), (1, 1)]
EMPTY = -1e30
F32 = jnp.float32
BF16 = jnp.bfloat16


def dot(a, b):
    return jnp.dot(a, b, preferred_element_type=F32)


def dot_nt(a, b):
    return lax.dot_general(a, b, (((1,), (1,)), ((), ())), preferred_element_type=F32)


def dot_tn(a, b):
    return lax.dot_general(a, b, (((0,), (0,)), ((), ())), preferred_element_type=F32)


ROW, COL, INVERSE, SCALE, PEAK, PEAKS = 5, 6, 7, 8, 9, 16


def derive(table, rows):
    index = lax.broadcasted_iota(jnp.int32, rows.shape, 0)
    powers = jnp.exp(jnp.where(index < BANDS, rows, jnp.where(index == 7, -rows, 0.0)))
    inverse = powers[7:8] * (1.0 / MARGIN)
    peak = inverse * (1.0 / math.sqrt(2.0 * math.pi))
    table[:7] = jnp.where(index < BANDS, powers, rows)[:7]
    table[INVERSE : INVERSE + 1] = inverse
    table[SCALE : SCALE + 1] = inverse * inverse * (-0.5 * math.log2(math.e))
    table[PEAK : PEAK + 1] = peak
    table[PEAKS : PEAKS + 8] = powers * peak


def row(table, i, lanes=slice(None)):
    if isinstance(i, int):
        return table[i : i + 1, lanes]
    return jnp.where(i == ROW, table[ROW : ROW + 1, lanes], table[COL : COL + 1, lanes])


def distance(first, count, center):
    return lax.broadcasted_iota(jnp.int32, (count, 1), 0).astype(F32) + first - center


def fill_long(ref, full, length, first, table, axis, step=32, width=128):
    for lo in range(0, ref.shape[1], width):
        lanes = slice(lo, lo + width)
        d0 = distance(first, step, row(table, axis, lanes))
        scale, peak = row(table, SCALE, lanes), row(table, PEAK, lanes)
        for r in range(0, length, step):
            d = d0 + float(r)
            p = jnp.exp2(d * (d * scale)) * peak
            full[r : r + step, lanes] = p
            ref[r : r + step, lanes] = p.astype(BF16)


def fill_scaled(ref, first, table, axis, step=32, width=128):
    for lo in range(0, ref.shape[1], width):
        lanes = slice(lo, lo + width)
        d0 = distance(first, step, row(table, axis, lanes))
        scale = row(table, SCALE, lanes)
        peaks = [row(table, PEAKS + b, lanes) for b in range(BANDS)]
        for r in range(0, MARGIN, step):
            d = d0 + float(r)
            e = jnp.exp2(d * (d * scale))
            for b in range(BANDS):
                ref[b * MARGIN + r : b * MARGIN + r + step, lanes] = (e * peaks[b]).astype(BF16)


def fold(x):
    total = x[:8]
    for i in range(8, x.shape[0], 8):
        total = total + x[i : i + 8]
    return total


def reduce_short(buf, first, table, axis, step=32, width=128):
    parts = []
    for lo in range(0, buf.shape[1], width):
        lanes = slice(lo, lo + width)
        fluxes = [row(table, b, lanes) for b in range(BANDS)]
        scale = row(table, SCALE, lanes)
        d0 = distance(first, step, row(table, axis, lanes))
        sums = None
        for r in range(0, MARGIN, step):
            d = d0 + float(r)
            e = jnp.exp2(d * (d * scale))
            new = []
            total = None
            for b in range(BANDS):
                a = buf[b * MARGIN + r : b * MARGIN + r + step, lanes] * e
                new.append(fold(a))
                a = a * fluxes[b]
                total = a if total is None else total + a
            q = total * d
            new.extend([fold(q), fold(q * d)])
            sums = new if sums is None else [s + v for s, v in zip(sums, new)]
        parts.append([s * f for s, f in zip(sums, fluxes)] + sums[BANDS:])
    return [jnp.concatenate([p[m] for p in parts], axis=1) for m in range(BANDS + 2)]


def reduce_long(buf, shape, length, first, table, axis, step=32, width=128):
    parts = []
    for lo in range(0, buf.shape[1], width):
        lanes = slice(lo, lo + width)
        d0 = distance(first, step, row(table, axis, lanes))
        sums = None
        for r in range(0, length, step):
            q = shape[r : r + step, lanes] * buf[r : r + step, lanes]
            d = d0 + float(r)
            q1 = q * d
            new = [fold(q), fold(q1), fold(q1 * d)]
            sums = new if sums is None else [s + v for s, v in zip(sums, new)]
        parts.append(sums)
    return [jnp.concatenate([p[m] for p in parts], axis=1) for m in range(3)]


def settle(short, long, table):
    peak, inverse = row(table, PEAK), row(table, INVERSE)
    short = [jnp.sum(v, axis=0, keepdims=True) * peak for v in short]
    long = [jnp.sum(v, axis=0, keepdims=True) for v in long]
    square = inverse * inverse
    bands = short[:BANDS]
    zeroth = bands[0] + bands[1] + bands[2] + bands[3] + bands[4]
    width = square * short[BANDS + 1] - zeroth + (square * long[2] - long[0])
    return bands, square * short[BANDS], square * long[1], width


def core(side, cap, arrived, sky, counts_hbm, leaving, prm, out, counts, canvas, w, rim_sum,
         c_sc, e_sc, e_long, k_sc, k_long, xa, xb, yb, yk, e_full, k_full, sem):
    M = MARGIN
    chunks = side // M
    last = side - M
    fetch = pltpu.make_async_copy(counts_hbm, counts, sem)
    fetch.start()
    tiles = arrived.shape[0] // 9
    slots = prm.shape[2]
    for n in range(9):
        table = arrived[pl.ds(n, tiles, stride=9), :].T
        derive(prm.at[n], jnp.concatenate([table[8 * r : 8 * r + 8] for r in range(cap)], axis=1))

    def number(c):
        return c.astype(F32) * float(M) + 0.5

    def rim_at(i):
        return side if i % 2 == 0 else -M

    own = prm.at[0]

    for c in range(chunks):
        rows = pl.ds(c * M, M)
        fill_long(e_long.at[0, rows, :], e_full.at[0, rows, :], M, c * M + 0.5, own, COL)

    for c in range(chunks):
        fill_scaled(c_sc.at[c], c * M + 0.5, own, ROW)
        canvas[c] = dot_nt(c_sc[c], e_long[0])
        if c < 4:
            across, along = (ROW, COL) if c < 2 else (COL, ROW)
            fill_scaled(e_sc.at[c], rim_at(c) + 0.5, prm.at[1 + c], across)
            fill_long(e_long.at[1 + c], e_full.at[1 + c], side, 0.5, prm.at[1 + c], along)
            fill_scaled(k_sc.at[c], rim_at(c) + 0.5, prm.at[5 + c], COL)
            fill_long(k_long.at[c], k_full.at[c], M, rim_at(c // 2) + 0.5, prm.at[5 + c], ROW)

    def rim_render(v, _):
        rim_sum[v] = dot_nt(e_long[3 + v], e_sc[2 + v])
        canvas[v * (chunks - 1)] += dot_nt(e_sc[v], e_long[1 + v])
        rim_sum[v, :M] += dot_nt(k_long[v], k_sc[v])
        rim_sum[v, last:] += dot_nt(k_long[2 + v], k_sc[2 + v])
        return 0

    for v in range(2):
        rim_render(v, 0)

    fetch.wait()

    def weigh(c, own):
        rows = slice(c * M, c * M + M)
        for b in range(BANDS):
            band = slice(b * M, (b + 1) * M)
            level = sky[0, 0, b]
            seen = counts[b, rows, :].astype(F32)
            left = canvas[c, band, :M] + rim_sum[0, rows, band]
            right = canvas[c, band, last:] + rim_sum[1, rows, band]
            model = jnp.concatenate([left, canvas[c, band, M:last], right], axis=1)
            weights = (seen / (model + level) - 1.0).astype(BF16)
            own[band, :] = weights
            w[chunks, band, rows] = weights[:, :M].T
            w[chunks + 1, band, rows] = weights[:, last:].T

    weigh(0, w.at[0])

    own_short = None
    for c in range(chunks):
        if c > 0:
            found = reduce_short(xa, (c - 1) * M + 0.5, own, ROW)
            own_short = found if own_short is None else [s + f for s, f in zip(own_short, found)]
        xa[...] = dot(w[c], e_long[0])
        if c < chunks - 1:
            weigh(c + 1, w.at[c + 1])
    both = lambda ref: ref[:chunks].reshape(chunks * BANDS * M, -1)
    yb[...] = dot_tn(both(w), both(c_sc))

    def settle_tile(g):
        table = prm.at[g]
        short_axis, long_axis = (ROW, COL) if g < 3 else (COL, ROW)
        first = (last if g == 0 else rim_at(g - 1)) + 0.5
        short = reduce_short(xa, first, table, short_axis)
        if g == 0:
            short = [s + h for s, h in zip(short, own_short)]
        long = reduce_long(yb, e_full.at[g], side, 0.5, table, long_axis)
        bands, across, along, width = settle(short, long, table)
        grads = [across, along] if g < 3 else [along, across]
        out[g] = jnp.concatenate(bands + grads + [width], axis=0)

    def settle_corner(k):
        table = prm.at[5 + k]
        found = reduce_short(xb, rim_at(k) + 0.5, table, COL)
        long = reduce_long(yk, k_full.at[k], M, rim_at(k // 2) + 0.5, table, ROW)
        bands, col_grad, row_grad, width = settle(found, long, table)
        out[5 + k] = jnp.concatenate(bands + [row_grad, col_grad, width], axis=0)

    for e in range(4):
        settle_tile(e)
        if e > 0:
            settle_corner(e - 1)
        strip = (0, chunks - 1, chunks, chunks + 1)[e]
        rim, at = chunks + e % 2, slice(e // 2 * last, e // 2 * last + M)
        xa[...] = dot(w[strip], e_long[1 + e])
        xb[...] = dot(w[rim, :, at], k_long[e])
        yk[...] = dot_tn(w[rim, :, at], k_sc[e])
        yb[...] = dot_tn(w[strip], e_sc[e])
    settle_corner(3)
    settle_tile(4)

    for n in range(9):
        found = out[n]
        rows = [found[:, r * tiles : (r + 1) * tiles] for r in range(cap)]
        if cap < 16:
            rows.append(jnp.zeros((128 - 8 * cap, tiles), F32))
        leaving[pl.ds(n, tiles, stride=9), :] = jnp.concatenate(rows, axis=0).T


def render_and_adjoin(arrived, sky_level, counts, cap):
    _, side, _ = counts.shape
    slots = arrived.shape[0] // 9 * cap
    M, B = MARGIN, BANDS
    chunks = side // M
    vm = lambda *s: pltpu.VMEM(s, BF16)
    vf = lambda *s: pltpu.VMEM(s, F32)
    scratch = [
        vf(9, 24, slots), vf(9, 8, slots), pltpu.VMEM(counts.shape, counts.dtype), vf(chunks, B * M, side),
        vm(chunks + 2, B * M, side), vf(2, side, B * M),
        vm(chunks, B * M, slots),
        vm(4, B * M, slots), vm(5, side, slots),
        vm(4, B * M, slots), vm(4, M, slots),
        vf(B * M, slots), vf(B * M, slots), vf(side, slots), vf(M, slots),
        vf(5, side, slots), vf(4, M, slots),
        pltpu.SemaphoreType.DMA,
    ]
    return pl.pallas_call(
        functools.partial(core, side, cap),
        out_shape=jax.ShapeDtypeStruct(arrived.shape, F32),
        in_specs=[
            pl.BlockSpec(memory_space=pltpu.VMEM),
            pl.BlockSpec(memory_space=pltpu.SMEM),
            pl.BlockSpec(memory_space=pl.ANY),
        ],
        out_specs=pl.BlockSpec(memory_space=pltpu.VMEM),
        scratch_shapes=scratch,
        compiler_params=pltpu.CompilerParams(vmem_limit_bytes=60 * 1024 * 1024),
    )(arrived, sky_level, counts)


def exact_dot(hot, values, contract):
    high = values.astype(BF16)
    rest = values - high.astype(F32)
    middle = rest.astype(BF16)
    low = (rest - middle.astype(F32)).astype(BF16)
    total = None
    for part in (low, middle, high):
        found = lax.dot_general(hot, part, (contract, ((), ())), preferred_element_type=F32)
        total = found if total is None else total + found
    return total


def ranks(owner_row):
    here = owner_row.shape[1]
    first = lax.broadcasted_iota(jnp.int32, (here, here), 0)
    second = lax.broadcasted_iota(jnp.int32, (here, here), 1)
    numbers = owner_row.astype(F32)
    column = jnp.broadcast_to(numbers, (8, here)).T[:, :1]
    same = (column == numbers) & (first < second)
    return jnp.sum(jnp.where(same, 1.0, 0.0), axis=0, keepdims=True).astype(jnp.int32)


def turned(x, shift):
    shift = shift % x.shape[0]
    return x if shift == 0 else jnp.concatenate([x[shift:], x[:shift]], axis=0)


def send_rows(n_ra, n_dec, cap, log_flux, position, log_width, owner, out):
    tiles = n_ra * n_dec
    here = owner.shape[1]
    owner_row = owner[...]
    rank_row = ranks(owner_row)
    rows = jnp.concatenate([log_flux[...], position[...], log_width[...]], axis=0)
    place = lax.broadcasted_iota(jnp.int32, (128, here), 0)
    mine = (place // 8 == rank_row) & (rank_row < cap)
    spread = jnp.where(mine, jnp.concatenate([rows] * 16, axis=0), 0.0)
    hot = (lax.broadcasted_iota(jnp.int32, (tiles, here), 0) == owner_row).astype(F32).astype(BF16)
    contract = ((1,), (1,))
    base = exact_dot(hot, spread, contract)
    taken = lax.dot_general(hot, mine.astype(F32).astype(BF16), (contract, ((), ())), preferred_element_type=F32)
    lane = lax.broadcasted_iota(jnp.int32, (tiles, 128), 1) % 8
    empty = jnp.where(lane < BANDS, EMPTY, 0.0)
    base = jnp.where(taken > 0.5, base, empty)
    tile = lax.broadcasted_iota(jnp.int32, (tiles, 1), 0)
    at_ra, at_dec = tile // n_dec, tile % n_dec
    for n, (i, j) in enumerate(AROUND):
        inside = (at_ra + i >= 0) & (at_ra + i < n_ra) & (at_dec + j >= 0) & (at_dec + j < n_dec)
        out[pl.ds(n, tiles, stride=9), :] = jnp.where(inside, turned(base, i * n_dec + j), empty)


def collect_rows(n_ra, n_dec, cap, arrived, owner, out):
    tiles = n_ra * n_dec
    here = owner.shape[1]
    owner_row = owner[...]
    rank_row = ranks(owner_row)
    total = None
    for n, (i, j) in enumerate(AROUND):
        part = turned(arrived[pl.ds(n, tiles, stride=9), :], -(i * n_dec + j))
        total = part if total is None else total + part
    hot = (lax.broadcasted_iota(jnp.int32, (tiles, here), 0) == owner_row).astype(F32).astype(BF16)
    picked = exact_dot(hot, total, ((0,), (0,))).T
    place = lax.broadcasted_iota(jnp.int32, (128, here), 0) // 8
    picked = jnp.where(place == rank_row, picked, 0.0)
    found = picked[:8]
    for r in range(1, cap):
        found = found + picked[8 * r : 8 * r + 8]
    out[...] = found


def on_device(log_flux, position, log_width, owner_tile, sky_level, counts):
    n_ra, n_dec = lax.axis_size("ra"), lax.axis_size("dec")
    tiles = n_ra * n_dec
    cap = max(2, 2 * CAT_DEV // tiles)
    here = log_flux.shape[1]
    owner = owner_tile.reshape(1, here)
    box = jax.ShapeDtypeStruct((9 * tiles, 128), F32)
    leaving = pl.pallas_call(functools.partial(send_rows, n_ra, n_dec, cap), out_shape=box)(
        log_flux, position, log_width[None, :], owner
    )
    arrived = lax.all_to_all(leaving.reshape(-1), AXES, split_axis=0, concat_axis=0, tiled=True)
    partial = render_and_adjoin(arrived.reshape(box.shape), sky_level, counts, cap)
    back = lax.all_to_all(partial.reshape(-1), AXES, split_axis=0, concat_axis=0, tiled=True)
    return pl.pallas_call(
        functools.partial(collect_rows, n_ra, n_dec, cap), out_shape=jax.ShapeDtypeStruct((8, here), F32)
    )(back.reshape(box.shape), owner)


def solution(mesh):
    in_specs = (
        P(None, AXES),
        P(None, AXES),
        P(AXES),
        P(AXES, None),
        P("ra", "dec", None),
        P(None, "ra", "dec"),
    )
    return jax.shard_map(
        on_device, mesh=mesh, in_specs=in_specs, out_specs=P(None, AXES), check_vma=False
    )
```

```python
import functools
import math

import jax
import jax.numpy as jnp
from jax import lax
from jax.experimental import pallas as pl
from jax.experimental.pallas import tpu as pltpu
from jax.sharding import PartitionSpec as P

MARGIN = 128
CAT_DEV = 256
BANDS = 5
AXES = ("ra", "dec")
AROUND = [(0, 0), (-1, 0), (1, 0), (0, -1), (0, 1), (-1, -1), (-1, 1), (1, -1), (1, 1)]
EMPTY = -1e30
F32 = jnp.float32
BF16 = jnp.bfloat16


def dot(a, b):
    return jnp.dot(a, b, preferred_element_type=F32)


def dot_nt(a, b):
    return lax.dot_general(a, b, (((1,), (1,)), ((), ())), preferred_element_type=F32)


def dot_tn(a, b):
    return lax.dot_general(a, b, (((0,), (0,)), ((), ())), preferred_element_type=F32)


ROW, COL, INVERSE, SCALE, PEAK, PEAKS = 5, 6, 7, 8, 9, 16


def derive(table, rows):
    index = lax.broadcasted_iota(jnp.int32, rows.shape, 0)
    powers = jnp.exp(jnp.where(index < BANDS, rows, jnp.where(index == 7, -rows, 0.0)))
    inverse = powers[7:8] * (1.0 / MARGIN)
    peak = inverse * (1.0 / math.sqrt(2.0 * math.pi))
    table[:7] = jnp.where(index < BANDS, powers, rows)[:7]
    table[INVERSE : INVERSE + 1] = inverse
    table[SCALE : SCALE + 1] = inverse * inverse * (-0.5 * math.log2(math.e))
    table[PEAK : PEAK + 1] = peak
    table[PEAKS : PEAKS + 8] = powers * peak


def row(table, i, lanes=slice(None)):
    if isinstance(i, int):
        return table[i : i + 1, lanes]
    return jnp.where(i == ROW, table[ROW : ROW + 1, lanes], table[COL : COL + 1, lanes])


def distance(first, count, center):
    return lax.broadcasted_iota(jnp.int32, (count, 1), 0).astype(F32) + first - center


def fill_long(ref, full, length, first, table, axis, step=32, width=128):
    for lo in range(0, ref.shape[1], width):
        lanes = slice(lo, lo + width)
        d0 = distance(first, step, row(table, axis, lanes))
        scale, peak = row(table, SCALE, lanes), row(table, PEAK, lanes)
        for r in range(0, length, step):
            d = d0 + float(r)
            p = jnp.exp2(d * (d * scale)) * peak
            full[r : r + step, lanes] = p
            ref[r : r + step, lanes] = p.astype(BF16)


def fill_scaled(ref, first, table, axis, step=32, width=128):
    for lo in range(0, ref.shape[1], width):
        lanes = slice(lo, lo + width)
        d0 = distance(first, step, row(table, axis, lanes))
        scale = row(table, SCALE, lanes)
        peaks = [row(table, PEAKS + b, lanes) for b in range(BANDS)]
        for r in range(0, MARGIN, step):
            d = d0 + float(r)
            e = jnp.exp2(d * (d * scale))
            for b in range(BANDS):
                ref[b * MARGIN + r : b * MARGIN + r + step, lanes] = (e * peaks[b]).astype(BF16)


def fold(x):
    total = x[:8]
    for i in range(8, x.shape[0], 8):
        total = total + x[i : i + 8]
    return total


def reduce_short(buf, first, table, axis, step=32, width=128):
    parts = []
    for lo in range(0, buf.shape[1], width):
        lanes = slice(lo, lo + width)
        fluxes = [row(table, b, lanes) for b in range(BANDS)]
        scale = row(table, SCALE, lanes)
        d0 = distance(first, step, row(table, axis, lanes))
        sums = None
        for r in range(0, MARGIN, step):
            d = d0 + float(r)
            e = jnp.exp2(d * (d * scale))
            new = []
            total = None
            for b in range(BANDS):
                a = buf[b * MARGIN + r : b * MARGIN + r + step, lanes] * e
                new.append(fold(a))
                a = a * fluxes[b]
                total = a if total is None else total + a
            q = total * d
            new.extend([fold(q), fold(q * d)])
            sums = new if sums is None else [s + v for s, v in zip(sums, new)]
        parts.append([s * f for s, f in zip(sums, fluxes)] + sums[BANDS:])
    return [jnp.concatenate([p[m] for p in parts], axis=1) for m in range(BANDS + 2)]


def reduce_long(buf, shape, length, first, table, axis, step=32, width=128):
    parts = []
    for lo in range(0, buf.shape[1], width):
        lanes = slice(lo, lo + width)
        d0 = distance(first, step, row(table, axis, lanes))
        sums = None
        for r in range(0, length, step):
            q = shape[r : r + step, lanes] * buf[r : r + step, lanes]
            d = d0 + float(r)
            q1 = q * d
            new = [fold(q), fold(q1), fold(q1 * d)]
            sums = new if sums is None else [s + v for s, v in zip(sums, new)]
        parts.append(sums)
    return [jnp.concatenate([p[m] for p in parts], axis=1) for m in range(3)]


def settle(short, long, table):
    peak, inverse = row(table, PEAK), row(table, INVERSE)
    short = [jnp.sum(v, axis=0, keepdims=True) * peak for v in short]
    long = [jnp.sum(v, axis=0, keepdims=True) for v in long]
    square = inverse * inverse
    bands = short[:BANDS]
    zeroth = bands[0] + bands[1] + bands[2] + bands[3] + bands[4]
    width = square * short[BANDS + 1] - zeroth + (square * long[2] - long[0])
    return bands, square * short[BANDS], square * long[1], width


def core(side, cap, arrived, sky, counts_hbm, leaving, prm, out, counts, canvas, w, rim_sum,
         c_sc, e_sc, e_long, k_sc, k_long, xa, xb, yb, yk, e_full, k_full, sem):
    M = MARGIN
    chunks = side // M
    last = side - M
    fetch = pltpu.make_async_copy(counts_hbm, counts, sem)
    fetch.start()
    tiles = arrived.shape[0] // 9
    slots = prm.shape[2]
    for n in range(9):
        table = arrived[pl.ds(n, tiles, stride=9), :].T
        derive(prm.at[n], jnp.concatenate([table[8 * r : 8 * r + 8] for r in range(cap)], axis=1))

    def number(c):
        return c.astype(F32) * float(M) + 0.5

    def rim_at(i):
        return side if i % 2 == 0 else -M

    own = prm.at[0]

    for c in range(chunks):
        rows = pl.ds(c * M, M)
        fill_long(e_long.at[0, rows, :], e_full.at[0, rows, :], M, c * M + 0.5, own, COL)

    for c in range(chunks):
        fill_scaled(c_sc.at[c], c * M + 0.5, own, ROW)
        canvas[c] = dot_nt(c_sc[c], e_long[0])
        if c < 4:
            across, along = (ROW, COL) if c < 2 else (COL, ROW)
            fill_scaled(e_sc.at[c], rim_at(c) + 0.5, prm.at[1 + c], across)
            fill_long(e_long.at[1 + c], e_full.at[1 + c], side, 0.5, prm.at[1 + c], along)
            fill_scaled(k_sc.at[c], rim_at(c) + 0.5, prm.at[5 + c], COL)
            fill_long(k_long.at[c], k_full.at[c], M, rim_at(c // 2) + 0.5, prm.at[5 + c], ROW)

    for v in range(2):
        rim_sum[v] = dot_nt(e_long[3 + v], e_sc[2 + v])
    for v in range(2):
        canvas[v * (chunks - 1)] += dot_nt(e_sc[v], e_long[1 + v])
        rim_sum[v, :M] += dot_nt(k_long[v], k_sc[v])
        rim_sum[v, last:] += dot_nt(k_long[2 + v], k_sc[2 + v])

    fetch.wait()

    def weigh(c, own):
        rows = slice(c * M, c * M + M)
        for b in range(BANDS):
            band = slice(b * M, (b + 1) * M)
            level = sky[0, 0, b]
            seen = counts[b, rows, :].astype(F32)
            left = canvas[c, band, :M] + rim_sum[0, rows, band]
            right = canvas[c, band, last:] + rim_sum[1, rows, band]
            model = jnp.concatenate([left, canvas[c, band, M:last], right], axis=1)
            weights = (seen / (model + level) - 1.0).astype(BF16)
            own[band, :] = weights
            w[chunks, band, rows] = weights[:, :M].T
            w[chunks + 1, band, rows] = weights[:, last:].T

    order = list(range(1, chunks - 1)) + [0, chunks - 1]
    weigh(order[0], w.at[order[0]])

    own_short = None
    for i, c in enumerate(order):
        if i > 0:
            found = reduce_short(xa, order[i - 1] * M + 0.5, own, ROW)
            own_short = found if own_short is None else [s + f for s, f in zip(own_short, found)]
        xa[...] = dot(w[c], e_long[0])
        if i < chunks - 1:
            weigh(order[i + 1], w.at[order[i + 1]])
    both = lambda ref: ref[:chunks].reshape(chunks * BANDS * M, -1)
    yb[...] = dot_tn(both(w), both(c_sc))

    def settle_tile(g):
        table = prm.at[g]
        short_axis, long_axis = (ROW, COL) if g < 3 else (COL, ROW)
        first = (last if g == 0 else rim_at(g - 1)) + 0.5
        short = reduce_short(xa, first, table, short_axis)
        if g == 0:
            short = [s + h for s, h in zip(short, own_short)]
        long = reduce_long(yb, e_full.at[g], side, 0.5, table, long_axis)
        bands, across, along, width = settle(short, long, table)
        grads = [across, along] if g < 3 else [along, across]
        out[g] = jnp.concatenate(bands + grads + [width], axis=0)

    def settle_corner(k):
        table = prm.at[5 + k]
        found = reduce_short(xb, rim_at(k) + 0.5, table, COL)
        long = reduce_long(yk, k_full.at[k], M, rim_at(k // 2) + 0.5, table, ROW)
        bands, col_grad, row_grad, width = settle(found, long, table)
        out[5 + k] = jnp.concatenate(bands + [row_grad, col_grad, width], axis=0)

    for e in range(4):
        settle_tile(e)
        if e > 0:
            settle_corner(e - 1)
        strip = (0, chunks - 1, chunks, chunks + 1)[e]
        rim, at = chunks + e % 2, slice(e // 2 * last, e // 2 * last + M)
        xa[...] = dot(w[strip], e_long[1 + e])
        xb[...] = dot(w[rim, :, at], k_long[e])
        yk[...] = dot_tn(w[rim, :, at], k_sc[e])
        yb[...] = dot_tn(w[strip], e_sc[e])
    settle_corner(3)
    settle_tile(4)

    for n in range(9):
        found = out[n]
        rows = [found[:, r * tiles : (r + 1) * tiles] for r in range(cap)]
        if cap < 16:
            rows.append(jnp.zeros((128 - 8 * cap, tiles), F32))
        leaving[pl.ds(n, tiles, stride=9), :] = jnp.concatenate(rows, axis=0).T


def render_and_adjoin(arrived, sky_level, counts, cap):
    _, side, _ = counts.shape
    slots = arrived.shape[0] // 9 * cap
    M, B = MARGIN, BANDS
    chunks = side // M
    vm = lambda *s: pltpu.VMEM(s, BF16)
    vf = lambda *s: pltpu.VMEM(s, F32)
    scratch = [
        vf(9, 24, slots), vf(9, 8, slots), pltpu.VMEM(counts.shape, counts.dtype), vf(chunks, B * M, side),
        vm(chunks + 2, B * M, side), vf(2, side, B * M),
        vm(chunks, B * M, slots),
        vm(4, B * M, slots), vm(5, side, slots),
        vm(4, B * M, slots), vm(4, M, slots),
        vf(B * M, slots), vf(B * M, slots), vf(side, slots), vf(M, slots),
        vf(5, side, slots), vf(4, M, slots),
        pltpu.SemaphoreType.DMA,
    ]
    return pl.pallas_call(
        functools.partial(core, side, cap),
        out_shape=jax.ShapeDtypeStruct(arrived.shape, F32),
        in_specs=[
            pl.BlockSpec(memory_space=pltpu.VMEM),
            pl.BlockSpec(memory_space=pltpu.SMEM),
            pl.BlockSpec(memory_space=pl.ANY),
        ],
        out_specs=pl.BlockSpec(memory_space=pltpu.VMEM),
        scratch_shapes=scratch,
        compiler_params=pltpu.CompilerParams(vmem_limit_bytes=60 * 1024 * 1024),
    )(arrived, sky_level, counts)


def exact_dot(hot, values, contract):
    high = values.astype(BF16)
    rest = values - high.astype(F32)
    middle = rest.astype(BF16)
    low = (rest - middle.astype(F32)).astype(BF16)
    total = None
    for part in (low, middle, high):
        found = lax.dot_general(hot, part, (contract, ((), ())), preferred_element_type=F32)
        total = found if total is None else total + found
    return total


def ranks(owner_row):
    here = owner_row.shape[1]
    first = lax.broadcasted_iota(jnp.int32, (here, here), 0)
    second = lax.broadcasted_iota(jnp.int32, (here, here), 1)
    numbers = owner_row.astype(F32)
    column = jnp.broadcast_to(numbers, (8, here)).T[:, :1]
    same = (column == numbers) & (first < second)
    return jnp.sum(jnp.where(same, 1.0, 0.0), axis=0, keepdims=True).astype(jnp.int32)


def turned(x, shift):
    shift = shift % x.shape[0]
    return x if shift == 0 else jnp.concatenate([x[shift:], x[:shift]], axis=0)


def send_rows(n_ra, n_dec, cap, log_flux, position, log_width, owner, out):
    tiles = n_ra * n_dec
    here = owner.shape[1]
    owner_row = owner[...]
    rank_row = ranks(owner_row)
    rows = jnp.concatenate([log_flux[...], position[...], log_width[...]], axis=0)
    place = lax.broadcasted_iota(jnp.int32, (128, here), 0)
    mine = (place // 8 == rank_row) & (rank_row < cap)
    spread = jnp.where(mine, jnp.concatenate([rows] * 16, axis=0), 0.0)
    hot = (lax.broadcasted_iota(jnp.int32, (tiles, here), 0) == owner_row).astype(F32).astype(BF16)
    contract = ((1,), (1,))
    base = exact_dot(hot, spread, contract)
    taken = lax.dot_general(hot, mine.astype(F32).astype(BF16), (contract, ((), ())), preferred_element_type=F32)
    lane = lax.broadcasted_iota(jnp.int32, (tiles, 128), 1) % 8
    empty = jnp.where(lane < BANDS, EMPTY, 0.0)
    base = jnp.where(taken > 0.5, base, empty)
    tile = lax.broadcasted_iota(jnp.int32, (tiles, 1), 0)
    at_ra, at_dec = tile // n_dec, tile % n_dec
    for n, (i, j) in enumerate(AROUND):
        inside = (at_ra + i >= 0) & (at_ra + i < n_ra) & (at_dec + j >= 0) & (at_dec + j < n_dec)
        out[pl.ds(n, tiles, stride=9), :] = jnp.where(inside, turned(base, i * n_dec + j), empty)


def collect_rows(n_ra, n_dec, cap, arrived, owner, out):
    tiles = n_ra * n_dec
    here = owner.shape[1]
    owner_row = owner[...]
    rank_row = ranks(owner_row)
    total = None
    for n, (i, j) in enumerate(AROUND):
        part = turned(arrived[pl.ds(n, tiles, stride=9), :], -(i * n_dec + j))
        total = part if total is None else total + part
    hot = (lax.broadcasted_iota(jnp.int32, (tiles, here), 0) == owner_row).astype(F32).astype(BF16)
    picked = exact_dot(hot, total, ((0,), (0,))).T
    place = lax.broadcasted_iota(jnp.int32, (128, here), 0) // 8
    picked = jnp.where(place == rank_row, picked, 0.0)
    found = picked[:8]
    for r in range(1, cap):
        found = found + picked[8 * r : 8 * r + 8]
    out[...] = found


def on_device(log_flux, position, log_width, owner_tile, sky_level, counts):
    n_ra, n_dec = lax.axis_size("ra"), lax.axis_size("dec")
    tiles = n_ra * n_dec
    cap = max(2, 2 * CAT_DEV // tiles)
    here = log_flux.shape[1]
    owner = owner_tile.reshape(1, here)
    box = jax.ShapeDtypeStruct((9 * tiles, 128), F32)
    leaving = pl.pallas_call(functools.partial(send_rows, n_ra, n_dec, cap), out_shape=box)(
        log_flux, position, log_width[None, :], owner
    )
    arrived = lax.all_to_all(leaving.reshape(-1), AXES, split_axis=0, concat_axis=0, tiled=True)
    partial = render_and_adjoin(arrived.reshape(box.shape), sky_level, counts, cap)
    back = lax.all_to_all(partial.reshape(-1), AXES, split_axis=0, concat_axis=0, tiled=True)
    return pl.pallas_call(
        functools.partial(collect_rows, n_ra, n_dec, cap), out_shape=jax.ShapeDtypeStruct((8, here), F32)
    )(back.reshape(box.shape), owner)


def solution(mesh):
    in_specs = (
        P(None, AXES),
        P(None, AXES),
        P(AXES),
        P(AXES, None),
        P("ra", "dec", None),
        P(None, "ra", "dec"),
    )
    return jax.shard_map(
        on_device, mesh=mesh, in_specs=in_specs, out_specs=P(None, AXES), check_vma=False
    )
```
